128 devices in a mesh: dp: 8 (over x, core), expert: 16 (over z, y).
Axes of the slice: x: 4, y: 4, z: 4, core: 2. Of those that a mesh axis runs over, the one named last changes fastest.
Arguments:
- coded: bfloat16 [16384, 2048], P(('dp', 'expert')), may hold values from -6 to 6
- block_scale: float32 [16384, 16], P(('dp', 'expert')), may hold values from 0.25 to 4
- routes: int32 [16384, 2], P(('dp', 'expert')), may hold values from 0 to 63, all different within a row; in each aligned block of 128 rows (0 to 127, 128 to 255, ...) at most 8 rows name the same one
- route_weight: float32 [16384, 2], P(('dp', 'expert')), may hold values from 0.2 to 1
- cotangent: bfloat16 [16384, 2048], P(('dp', 'expert')), may hold values from -6 to 6
- w_gate: bfloat16 [128, 2048, 704], P(('dp', 'expert')), may hold values from -0.125 to 0.125
- w_up: bfloat16 [128, 2048, 704], P(('dp', 'expert')), may hold values from -0.125 to 0.125
- w_down: bfloat16 [128, 704, 2048], P(('dp', 'expert')), may hold values from -0.15625 to 0.15625
Outputs:
- layer_out: bfloat16 [16384, 2048], P(('dp', 'expert'))
- grad_input: bfloat16 [16384, 2048], P(('dp', 'expert'))
- grad_weight: float32 [16384, 2], P(('dp', 'expert'))
- grad_gate: bfloat16 [128, 2048, 704], P(('dp', 'expert'))
- grad_up: bfloat16 [128, 2048, 704], P(('dp', 'expert'))
- grad_down: bfloat16 [128, 704, 2048], P(('dp', 'expert'))
The draws below stay inside these ranges and needn't reach their ends.
Inputs may be any that keep to these rules, and one draw needn't show every extreme that they name: The two experts of a token differ. Among the routes of the tokens of one device (aligned blocks of 128 tokens) at most 8 name one expert, and some block of every draw has exactly 8 routes to one expert.
All inputs are finite; a program needn't handle non-finite values.
Results may differ from the reference program's by a relative error of at most 0.0079.
Values may be sent and summed in bfloat16 or wider, within the bound.
No kernel may reach another device: no remote copies, remote signals or barrier semaphores. Data moves between devices by JAX's collectives and lax.ppermute only.
A program may use at most 128 MiB of HBM per device.

```python
import math
import jax
import jax.numpy as jnp
import numpy as np
from jax import lax

D = 2048
FF = 1408
BLOCK = 128
TOK_DEV = 128
EXPERTS = 64
HALF = 704
CAP = 8
TOKENS = 16384
N_DP = 8
N_EXPERT = 16


def level_of(rng, shape, shards, least, high):
    loudness = 1.0
    for dim, parts in shards:
        heights = jax.random.uniform(jax.random.fold_in(jax.random.fold_in(rng, 6), dim), (parts,), jnp.float32, least / len(shards), high / len(shards))
        loudness = loudness * jnp.repeat(jnp.exp(heights), shape[dim] // parts).reshape((-1,) + (1,) * (len(shape) - 1 - dim))
    return loudness


def deal_out(own_key, own, number, rows, count, top, limit, skew):
    sequence = jax.random.permutation(own_key, count)
    packed, common = load_shares(count, rows * top, limit, skew, True), load_shares(count, rows * top, limit, skew, False)
    places = jnp.arange(count)

    def named(lengths, turn):
        used = int((lengths > 0).sum())
        fixed = max(1, used // 4)
        moved = fixed + (places - fixed + turn * (used - fixed)) % max(1, count - fixed)
        return jnp.zeros((count,), jnp.int32).at[sequence[jnp.where(places < fixed, places, moved)]].set(jnp.asarray(lengths, jnp.int32))

    lengths = jnp.where(number % 4 == 0, named(packed, number // 4), named(common, number - number // 4 - 1))
    mixed = jax.random.permutation(jax.random.fold_in(own, 3), count)
    source_of, receiver = mixed[0:count // 2 * 2:2], mixed[1:count // 2 * 2:2]
    room = jnp.minimum(lengths[source_of] - 1, limit - lengths[receiver]) // 2
    room = jnp.where((source_of == sequence[0]) | (receiver == sequence[0]) | (lengths[receiver] == 0), 0, jnp.maximum(room, 0))
    moved = jax.random.randint(jax.random.fold_in(own, 4), (count // 2,), 0, 1 << 20) % (room + 1)
    lengths = lengths.at[source_of].add(-moved).at[receiver].add(moved)
    labels = jnp.searchsorted(jnp.cumsum(lengths), jnp.arange(rows * top), side="right").astype(jnp.int32)
    table = labels.reshape(top, rows).T
    table = table[jax.random.permutation(jax.random.fold_in(own, 1), rows)]
    turn = jax.random.randint(jax.random.fold_in(own, 2), (rows, 1), 0, top)
    return jnp.take_along_axis(table, (jnp.arange(top)[None, :] + turn) % top, axis=1)


def load_shares(count, total, limit, skew, full):
    weights = [(1 << 20) // math.isqrt(standing ** skew) + 1 for standing in range(1, count + 1)]
    largest = limit if full else min(limit, max(-(-total // count), total * weights[0] // sum(weights)))
    least = 1 if total - largest >= count - 1 else 0
    counts, spare = [largest] + [least] * (count - 1), total - largest - least * (count - 1)
    while spare > 0:
        candidates = [i for i in range(1, count) if counts[i] < largest] or [i for i in range(1, count) if counts[i] < limit]
        mass, budget = sum([weights[i] for i in candidates]), spare
        for i in candidates:
            extra = min(limit - counts[i], max(1, budget * weights[i] // mass), spare)
            counts[i] = counts[i] + extra
            spare = spare - extra
    return np.array(counts)


def gaussian(own_key, dims, spread, reach, cuts=(), kind=jnp.bfloat16):
    array = spread * jax.random.normal(own_key, dims, jnp.float32)
    if cuts:
        array = array * level_of(own_key, dims, cuts, -0.22, 0.18)
    return jnp.clip(array, -reach, reach).astype(kind)


def setup_inputs(seed: int = 0) -> dict:
    key_list = jax.random.split(jax.random.key(seed), 9)
    coded = gaussian(key_list[0], (TOKENS, D), 1.0, 6.0, ((0, 128),))
    block_scale = jnp.clip(jnp.exp(math.log(4.0) - 2.7725887 * jax.random.uniform(key_list[1], (TOKENS, D // BLOCK), jnp.float32) ** level_of(key_list[1], (TOKENS, D // BLOCK), ((0, 128),), -0.2, 0.2)), 0.25, 4.0)
    routes_keys = jax.random.split(jax.random.fold_in(key_list[2], 1), TOKENS // TOK_DEV)
    routes_turns = jax.random.permutation(jax.random.fold_in(key_list[2], 3), TOKENS // TOK_DEV)
    routes = jax.vmap(lambda own, number: deal_out(jax.random.fold_in(key_list[2], 2), own, number, TOK_DEV, EXPERTS, 2, CAP, 2))(routes_keys, routes_turns).reshape((TOKENS, 2))
    route_weight = jnp.clip(0.2 + 0.8 * jax.random.uniform(key_list[3], (TOKENS, 2), jnp.float32) ** level_of(key_list[3], (TOKENS, 2), ((0, 128),), -0.2, 0.2), 0.2, 1.0)
    cotangent = gaussian(key_list[4], (TOKENS, D), 1.0, 6.0, ((0, 128),))
    w_gate = gaussian(key_list[5], (2 * EXPERTS, D, HALF), D ** -0.5, 0.125, ((0, 128),))
    w_up = gaussian(key_list[6], (2 * EXPERTS, D, HALF), D ** -0.5, 0.125, ((0, 128),))
    w_down = gaussian(key_list[7], (2 * EXPERTS, HALF, D), FF ** -0.5, 0.15625, ((0, 128),))
    return {"coded": coded, "block_scale": block_scale, "routes": routes, "route_weight": route_weight, "cotangent": cotangent, "w_gate": w_gate, "w_up": w_up, "w_down": w_down}


def expert_pass(rows, cot_rows, gate_w, up_w, down_w):
    gate = jnp.dot(rows, gate_w, preferred_element_type=jnp.float32)
    upper = jnp.dot(rows, up_w, preferred_element_type=jnp.float32)
    sigma = jax.nn.sigmoid(gate)
    active = gate * sigma
    hidden = (active * upper).astype(jnp.bfloat16)
    partial_out = jnp.dot(hidden, down_w, preferred_element_type=jnp.float32)
    d_hidden = lax.dot_general(cot_rows, down_w, (((1,), (1,)), ((), ())), preferred_element_type=jnp.float32)
    d_upper = (d_hidden * active).astype(jnp.bfloat16)
    d_gate = (d_hidden * upper * sigma * (1.0 + gate * (1.0 - sigma))).astype(jnp.bfloat16)
    grad_down = lax.dot_general(hidden, cot_rows, (((0,), (0,)), ((), ())), preferred_element_type=jnp.float32).astype(jnp.bfloat16)
    grad_gate = lax.dot_general(rows, d_gate, (((0,), (0,)), ((), ())), preferred_element_type=jnp.float32).astype(jnp.bfloat16)
    grad_up = lax.dot_general(rows, d_upper, (((0,), (0,)), ((), ())), preferred_element_type=jnp.float32).astype(jnp.bfloat16)
    partial_in = lax.dot_general(d_gate, gate_w, (((1,), (1,)), ((), ())), preferred_element_type=jnp.float32)
    partial_in = partial_in + lax.dot_general(d_upper, up_w, (((1,), (1,)), ((), ())), preferred_element_type=jnp.float32)
    return partial_out, partial_in, grad_gate, grad_up, grad_down


def reference(coded, block_scale, routes, route_weight, cotangent, w_gate, w_up, w_down):
    nodes = N_DP * N_EXPERT
    count = 2 * TOK_DEV
    blocks = D // BLOCK
    inputs = (coded.astype(jnp.float32).reshape(TOKENS, blocks, BLOCK) * block_scale[:, :, None]).reshape(TOKENS, D).astype(jnp.bfloat16)
    route_cot = (route_weight.reshape(-1)[:, None] * jnp.repeat(cotangent.astype(jnp.float32), 2, axis=0)).astype(jnp.bfloat16)
    in_route = jnp.repeat(inputs, 2, axis=0)
    zero_row = jnp.zeros((1, D), jnp.bfloat16)
    in_padded = jnp.concatenate([in_route, zero_row], axis=0)
    cot_padded = jnp.concatenate([route_cot, zero_row], axis=0)
    local = routes.reshape(nodes, count)

    def table_of(device_routes, base):
        onehot = (device_routes[:, None] == jnp.arange(EXPERTS, dtype=jnp.int32)[None, :]).astype(jnp.int32)
        before = jnp.cumsum(onehot, axis=0) - onehot
        slot = jnp.sum(before * onehot, axis=1)
        position = device_routes * CAP + slot
        empty = jnp.full((EXPERTS * CAP,), nodes * count, jnp.int32)
        return empty.at[position].set(base + jnp.arange(count, dtype=jnp.int32))

    tables = jax.vmap(table_of)(local, jnp.arange(nodes, dtype=jnp.int32) * count)
    tables = tables.reshape(nodes, EXPERTS, CAP).transpose(1, 0, 2).reshape(EXPERTS, nodes * CAP)

    def per_expert(operands):
        index, table = operands
        rows = in_padded[table]
        cots = cot_padded[table]
        first = expert_pass(rows, cots, w_gate[2 * index], w_up[2 * index], w_down[2 * index])
        second = expert_pass(rows, cots, w_gate[2 * index + 1], w_up[2 * index + 1], w_down[2 * index + 1])
        out_rows = (first[0].astype(jnp.bfloat16).astype(jnp.float32) + second[0].astype(jnp.bfloat16).astype(jnp.float32)).astype(jnp.bfloat16)
        in_rows = (first[1].astype(jnp.bfloat16).astype(jnp.float32) + second[1].astype(jnp.bfloat16).astype(jnp.float32)).astype(jnp.bfloat16)
        grads = tuple(jnp.stack([first[k], second[k]]) for k in (2, 3, 4))
        return out_rows, in_rows, grads[0], grads[1], grads[2]

    out_rows, in_rows, grad_gate, grad_up, grad_down = lax.map(per_expert, (jnp.arange(EXPERTS, dtype=jnp.int32), tables))
    flat_table = tables.reshape(-1)
    expert_out = jnp.zeros((nodes * count, D), jnp.bfloat16).at[flat_table].set(out_rows.reshape(-1, D), mode="drop")
    route_in = jnp.zeros((nodes * count, D), jnp.bfloat16).at[flat_table].set(in_rows.reshape(-1, D), mode="drop")
    expert_out = expert_out.reshape(TOKENS, 2, D).astype(jnp.float32)
    layer_out = jnp.sum(expert_out * route_weight[:, :, None], axis=1).astype(jnp.bfloat16)
    grad_input = jnp.sum(route_in.reshape(TOKENS, 2, D).astype(jnp.float32), axis=1).astype(jnp.bfloat16)
    grad_weight = jnp.sum(cotangent.astype(jnp.float32)[:, None, :] * expert_out, axis=2)
    return (layer_out, grad_input, grad_weight, grad_gate.reshape(2 * EXPERTS, D, HALF), grad_up.reshape(2 * EXPERTS, D, HALF), grad_down.reshape(2 * EXPERTS, HALF, D))
```

```python
import jax
import jax.numpy as jnp
from jax import lax
from jax.experimental import pallas as pl
from jax.experimental.pallas import tpu as pltpu
from jax.sharding import PartitionSpec as P

AXES = ("dp", "expert")
CAP = 8
VMEM_LIMIT = 48 * 1024 * 1024


def row_to_column(row, size):
    eye = lax.broadcasted_iota(jnp.int32, (size, size), 0) == lax.broadcasted_iota(jnp.int32, (size, size), 1)
    return jnp.sum(jnp.where(eye, row, 0.0), axis=1, keepdims=True)


def column_to_row(column, size):
    eye = lax.broadcasted_iota(jnp.int32, (size, size), 0) == lax.broadcasted_iota(jnp.int32, (size, size), 1)
    return jnp.sum(jnp.where(eye, column, 0.0), axis=0, keepdims=True)


def plan_kernel(experts, tokens, routes_ref, weight_ref, pick_ref, slot_weight_ref, position_ref):
    numbers = lax.broadcasted_iota(jnp.int32, (experts, tokens), 0)
    first = routes_ref[0:1, :] == numbers
    second = routes_ref[1:2, :] == numbers
    named = jnp.where(first | second, 1.0, 0.0)
    earlier = lax.broadcasted_iota(jnp.int32, (tokens, tokens), 0) < lax.broadcasted_iota(jnp.int32, (tokens, tokens), 1)
    rank = jnp.dot(
        named.astype(jnp.bfloat16),
        jnp.where(earlier, 1.0, 0.0).astype(jnp.bfloat16),
        preferred_element_type=jnp.float32,
    )
    weight = jnp.where(first, weight_ref[0:1, :], 0.0) + jnp.where(second, weight_ref[1:2, :], 0.0)
    slots = lax.broadcasted_iota(jnp.int32, (experts, CAP, tokens), 1).astype(jnp.float32)
    slot_of = jnp.where(named > 0.0, rank, -1.0)
    pick = jnp.broadcast_to(slot_of[:, None, :], (experts, CAP, tokens)) == slots
    pick_ref[...] = jnp.where(pick, 1.0, 0.0).astype(jnp.bfloat16).reshape(experts * CAP, tokens)
    spread = jnp.broadcast_to(weight[:, None, :], (experts, CAP, tokens))
    slot_weight_ref[...] = jnp.sum(jnp.where(pick, spread, 0.0).reshape(experts * CAP, tokens), axis=1, keepdims=True)
    place = numbers.astype(jnp.float32) * CAP + rank
    position_ref[0:1, :] = jnp.sum(jnp.where(first, place, 0.0), axis=0, keepdims=True).astype(jnp.int32)
    position_ref[1:2, :] = jnp.sum(jnp.where(second, place, 0.0), axis=0, keepdims=True).astype(jnp.int32)


def plan(routes, weight):
    tokens = routes.shape[1]
    experts = tokens // 2
    return pl.pallas_call(
        lambda *refs: plan_kernel(experts, tokens, *refs),
        out_shape=(
            jax.ShapeDtypeStruct((experts * CAP, tokens), jnp.bfloat16),
            jax.ShapeDtypeStruct((experts * CAP, 1), jnp.float32),
            jax.ShapeDtypeStruct((2, tokens), jnp.int32),
        ),
        name="plan",
    )(routes, weight)


def send_in_kernel(coded_ref, scale_ref, pick_ref, out_ref, inputs_ref):
    tokens, width = coded_ref.shape
    blocks = scale_ref.shape[0]
    size = width // blocks

    @pl.when(pl.program_id(0) == 0)
    def _():
        for b in range(blocks):
            columns = pl.ds(b * size, size)
            scale = row_to_column(scale_ref[b : b + 1, :], tokens)
            inputs_ref[:, columns] = (coded_ref[:, columns].astype(jnp.float32) * scale).astype(jnp.bfloat16)

    rows = jnp.dot(pick_ref[...], inputs_ref[...], preferred_element_type=jnp.float32).astype(jnp.bfloat16)
    rows = rows.reshape(-1, CAP, width)
    out_ref[:, 0] = rows
    out_ref[:, 1] = rows


def send_in(coded, scale, pick, steps=4):
    tokens, width = coded.shape
    experts = pick.shape[0] // CAP
    return pl.pallas_call(
        send_in_kernel,
        grid=(steps,),
        in_specs=[
            pl.BlockSpec(coded.shape, lambda i: (0, 0)),
            pl.BlockSpec(scale.shape, lambda i: (0, 0)),
            pl.BlockSpec((experts * CAP // steps, tokens), lambda i: (i, 0)),
        ],
        out_specs=pl.BlockSpec((experts // steps, 2, CAP, width), lambda i: (i, 0, 0, 0)),
        out_shape=jax.ShapeDtypeStruct((experts, 2, CAP, width), jnp.bfloat16),
        scratch_shapes=[pltpu.VMEM((tokens, width), jnp.bfloat16)],
        compiler_params=pltpu.CompilerParams(vmem_limit_bytes=VMEM_LIMIT),
        name="send_in",
    )(coded, scale, pick)


def send_cot_kernel(cot_ref, pick_ref, weight_ref, out_ref):
    rows = jnp.dot(pick_ref[...], cot_ref[...], preferred_element_type=jnp.float32)
    rows = (rows * weight_ref[...]).astype(jnp.bfloat16).reshape(-1, CAP, cot_ref.shape[1])
    out_ref[:, 0] = rows
    out_ref[:, 1] = rows


def send_cot(cotangent, pick, slot_weight, steps=4):
    tokens, width = cotangent.shape
    experts = pick.shape[0] // CAP
    return pl.pallas_call(
        send_cot_kernel,
        grid=(steps,),
        in_specs=[
            pl.BlockSpec(cotangent.shape, lambda i: (0, 0)),
            pl.BlockSpec((experts * CAP // steps, tokens), lambda i: (i, 0)),
            pl.BlockSpec((experts * CAP // steps, 1), lambda i: (i, 0)),
        ],
        out_specs=pl.BlockSpec((experts // steps, 2, CAP, width), lambda i: (i, 0, 0, 0)),
        out_shape=jax.ShapeDtypeStruct((experts, 2, CAP, width), jnp.bfloat16),
        compiler_params=pltpu.CompilerParams(vmem_limit_bytes=VMEM_LIMIT),
        cost_estimate=pl.CostEstimate(flops=2 * experts * CAP * tokens * width, bytes_accessed=10_000_000, transcendentals=0),
        name="send_cot",
    )(cotangent, pick, slot_weight)


def pair_rows(back_ref):
    both = back_ref[:, 0].astype(jnp.float32) + back_ref[:, 1].astype(jnp.float32)
    experts, cap, width = both.shape
    return both.reshape(experts * cap, width).astype(jnp.bfloat16)


def gather_rows(position, rows):
    numbers = lax.broadcasted_iota(jnp.int32, (rows.shape[0], position.shape[1]), 0)
    hit = jnp.where(numbers == position, 1.0, 0.0).astype(jnp.bfloat16)
    return lax.dot_general(hit, rows, (((0,), (0,)), ((), ())), preferred_element_type=jnp.float32)


def finish_out_kernel(back_ref, position_ref, weight_ref, cot_ref, out_ref, grad_ref):
    tokens = position_ref.shape[1]
    rows = pair_rows(back_ref)
    first = gather_rows(position_ref[0:1, :], rows)
    second = gather_rows(position_ref[1:2, :], rows)
    cot = cot_ref[...].astype(jnp.float32)
    total = first * row_to_column(weight_ref[0:1, :], tokens) + second * row_to_column(weight_ref[1:2, :], tokens)
    out_ref[...] = total.astype(jnp.bfloat16)

    @pl.when(pl.program_id(0) == 0)
    def _():
        grad_ref[...] = jnp.zeros_like(grad_ref)

    grad_ref[0:1, :] += column_to_row(jnp.sum(cot * first, axis=1, keepdims=True), tokens)
    grad_ref[1:2, :] += column_to_row(jnp.sum(cot * second, axis=1, keepdims=True), tokens)


def finish_out(back, position, weight, cotangent, steps=4):
    experts, _, cap, width = back.shape
    tokens = cotangent.shape[0]
    part = width // steps
    return pl.pallas_call(
        finish_out_kernel,
        grid=(steps,),
        in_specs=[
            pl.BlockSpec((experts, 2, cap, part), lambda i: (0, 0, 0, i)),
            pl.BlockSpec(position.shape, lambda i: (0, 0)),
            pl.BlockSpec(weight.shape, lambda i: (0, 0)),
            pl.BlockSpec((tokens, part), lambda i: (0, i)),
        ],
        out_specs=(
            pl.BlockSpec((tokens, part), lambda i: (0, i)),
            pl.BlockSpec((2, tokens), lambda i: (0, 0)),
        ),
        out_shape=(
            jax.ShapeDtypeStruct((tokens, width), jnp.bfloat16),
            jax.ShapeDtypeStruct((2, tokens), jnp.float32),
        ),
        compiler_params=pltpu.CompilerParams(vmem_limit_bytes=VMEM_LIMIT),
        cost_estimate=pl.CostEstimate(flops=4 * experts * cap * tokens * width, bytes_accessed=10_000_000, transcendentals=0),
        name="finish_out",
    )(back, position, weight, cotangent)


def finish_in_kernel(back_ref, position_ref, out_ref):
    rows = pair_rows(back_ref)
    total = gather_rows(position_ref[0:1, :], rows) + gather_rows(position_ref[1:2, :], rows)
    out_ref[...] = total.astype(jnp.bfloat16)


def finish_in(back, position, steps=4):
    experts, _, cap, width = back.shape
    tokens = position.shape[1]
    part = width // steps
    return pl.pallas_call(
        finish_in_kernel,
        grid=(steps,),
        in_specs=[
            pl.BlockSpec((experts, 2, cap, part), lambda i: (0, 0, 0, i)),
            pl.BlockSpec(position.shape, lambda i: (0, 0)),
        ],
        out_specs=pl.BlockSpec((tokens, part), lambda i: (0, i)),
        out_shape=jax.ShapeDtypeStruct((tokens, width), jnp.bfloat16),
        compiler_params=pltpu.CompilerParams(vmem_limit_bytes=VMEM_LIMIT),
        name="finish_in",
    )(back, position)


def dot(a, b, a_dim, b_dim):
    return lax.dot_general(a, b, (((a_dim,), (b_dim,)), ((), ())), preferred_element_type=jnp.float32)


def exchange(rows):
    return lax.all_to_all(rows, AXES, split_axis=0, concat_axis=0, tiled=True)


def on_device(coded, block_scale, routes, route_weight, cotangent, w_gate, w_up, w_down):
    tokens, width = coded.shape
    nodes = lax.axis_size(AXES)
    weight = route_weight.T
    gate_w, up_w, down_w = w_gate[0].T, w_up[0].T, w_down[0]

    pick, slot_weight, position = plan(routes.T, weight)
    rows = exchange(send_in(coded, block_scale.T, pick).reshape(nodes, CAP, width))
    cot_rows = exchange(send_cot(cotangent, pick, slot_weight).reshape(nodes, CAP, width))
    rows = rows.reshape(-1, width)
    cot_rows = cot_rows.reshape(-1, width)

    gate = dot(rows, gate_w, 1, 1)
    upper = dot(rows, up_w, 1, 1)
    sigma = jax.nn.sigmoid(gate)
    active = gate * sigma
    hidden = (active * upper).astype(jnp.bfloat16)
    partial_out = dot(hidden, down_w, 1, 0).astype(jnp.bfloat16)
    back_out = exchange(partial_out.reshape(nodes, CAP, width))

    d_hidden = dot(cot_rows, down_w, 1, 1)
    d_upper = (d_hidden * active).astype(jnp.bfloat16)
    d_gate = (d_hidden * upper * sigma * (1.0 + gate * (1.0 - sigma))).astype(jnp.bfloat16)
    partial_in = (dot(d_gate, gate_w, 1, 0) + dot(d_upper, up_w, 1, 0)).astype(jnp.bfloat16)
    back_in = exchange(partial_in.reshape(nodes, CAP, width))

    grad_down = dot(hidden, cot_rows, 0, 0).astype(jnp.bfloat16)
    grad_gate = dot(d_gate, rows, 0, 0).astype(jnp.bfloat16)
    grad_up = dot(d_upper, rows, 0, 0).astype(jnp.bfloat16)

    back_out = back_out.reshape(nodes // 2, 2, CAP, width)
    back_in = back_in.reshape(nodes // 2, 2, CAP, width)
    layer_out, grad_weight = finish_out(back_out, position, weight, cotangent)
    grad_input = finish_in(back_in, position)
    return (layer_out, grad_input, grad_weight.T, grad_gate.T[None], grad_up.T[None], grad_down[None])


def solution(mesh):
    rows = P(AXES, None)
    matrix = P(AXES, None, None)
    return jax.shard_map(
        on_device,
        mesh=mesh,
        in_specs=(rows, rows, rows, rows, rows, matrix, matrix, matrix),
        out_specs=(rows, rows, rows, matrix, matrix, matrix),
        check_vma=False,
    )
```

```python
import jax
import jax.numpy as jnp
from jax import lax
from jax.experimental import pallas as pl
from jax.experimental.pallas import tpu as pltpu
from jax.sharding import PartitionSpec as P

AXES = ("dp", "expert")
CAP = 8
VMEM_LIMIT = 60 * 1024 * 1024


def row_to_column(row, size):
    eye = lax.broadcasted_iota(jnp.int32, (size, size), 0) == lax.broadcasted_iota(jnp.int32, (size, size), 1)
    return jnp.sum(jnp.where(eye, row, 0.0), axis=1, keepdims=True)


def column_to_row(column, size):
    eye = lax.broadcasted_iota(jnp.int32, (size, size), 0) == lax.broadcasted_iota(jnp.int32, (size, size), 1)
    return jnp.sum(jnp.where(eye, column, 0.0), axis=0, keepdims=True)


def prepare_kernel(coded_hbm, scale_ref, routes_ref, weight_ref, out_ref, pick_ref, slot_weight_ref, place_ref, coded_ref, inputs_ref, sem):
    tokens, width = coded_ref.shape
    blocks = scale_ref.shape[0]
    size = width // blocks
    experts = tokens // 2
    part = out_ref.shape[0] * CAP
    step = pl.program_id(0)

    @pl.when(step == 0)
    def _():
        copy = pltpu.make_async_copy(coded_hbm, coded_ref, sem)
        copy.start()
        numbers = lax.broadcasted_iota(jnp.int32, (experts, tokens), 0)
        first = routes_ref[0:1, :] == numbers
        second = routes_ref[1:2, :] == numbers
        named = jnp.where(first | second, 1.0, 0.0)
        earlier = lax.broadcasted_iota(jnp.int32, (tokens, tokens), 0) < lax.broadcasted_iota(jnp.int32, (tokens, tokens), 1)
        rank = jnp.dot(
            named.astype(jnp.bfloat16),
            jnp.where(earlier, 1.0, 0.0).astype(jnp.bfloat16),
            preferred_element_type=jnp.float32,
        )
        weight = jnp.where(first, weight_ref[0:1, :], 0.0) + jnp.where(second, weight_ref[1:2, :], 0.0)
        slots = lax.broadcasted_iota(jnp.int32, (experts, CAP, tokens), 1).astype(jnp.float32)
        slot_of = jnp.where(named > 0.0, rank, -1.0)
        pick = jnp.broadcast_to(slot_of[:, None, :], (experts, CAP, tokens)) == slots
        pick_ref[...] = jnp.where(pick, 1.0, 0.0).astype(jnp.bfloat16).reshape(experts * CAP, tokens)
        spread = jnp.broadcast_to(weight[:, None, :], (experts, CAP, tokens))
        slot_weight_ref[...] = jnp.sum(jnp.where(pick, spread, 0.0).reshape(experts * CAP, tokens), axis=1, keepdims=True)
        place = numbers.astype(jnp.float32) * (2 * CAP) + rank
        place_ref[0:1, :] = jnp.sum(jnp.where(first, place, 0.0), axis=0, keepdims=True)
        place_ref[1:2, :] = jnp.sum(jnp.where(second, place, 0.0), axis=0, keepdims=True)
        copy.wait()
        for b in range(blocks):
            columns = pl.ds(b * size, size)
            scale = row_to_column(scale_ref[b : b + 1, :], tokens)
            inputs_ref[:, columns] = (coded_ref[:, columns].astype(jnp.float32) * scale).astype(jnp.bfloat16)

    pick = pick_ref[pl.ds(pl.multiple_of(step * part, part), part), :]
    rows = jnp.dot(pick, inputs_ref[...], preferred_element_type=jnp.float32).astype(jnp.bfloat16)
    rows = rows.reshape(-1, CAP, width)
    out_ref[:, 0] = rows
    out_ref[:, 1] = rows


def prepare(coded, scale, routes, weight, steps=4):
    tokens, width = coded.shape
    experts = tokens // 2
    whole = lambda i: (0, 0)
    return pl.pallas_call(
        prepare_kernel,
        grid=(steps,),
        in_specs=[
            pl.BlockSpec(memory_space=pl.ANY),
            pl.BlockSpec(scale.shape, whole),
            pl.BlockSpec(routes.shape, whole),
            pl.BlockSpec(weight.shape, whole),
        ],
        out_specs=(
            pl.BlockSpec((experts // steps, 2, CAP, width), lambda i: (i, 0, 0, 0)),
            pl.BlockSpec((experts * CAP, tokens), whole),
            pl.BlockSpec((experts * CAP, 1), whole),
            pl.BlockSpec((2, tokens), whole),
        ),
        out_shape=(
            jax.ShapeDtypeStruct((experts, 2, CAP, width), jnp.bfloat16),
            jax.ShapeDtypeStruct((experts * CAP, tokens), jnp.bfloat16),
            jax.ShapeDtypeStruct((experts * CAP, 1), jnp.float32),
            jax.ShapeDtypeStruct((2, tokens), jnp.float32),
        ),
        scratch_shapes=[
            pltpu.VMEM((tokens, width), jnp.bfloat16),
            pltpu.VMEM((tokens, width), jnp.bfloat16),
            pltpu.SemaphoreType.DMA(()),
        ],
        compiler_params=pltpu.CompilerParams(vmem_limit_bytes=VMEM_LIMIT),
        name="prepare",
    )(coded, scale, routes, weight)


def select_kernel(place_ref, first_ref, second_ref, both_ref):
    tokens = place_ref.shape[1]
    rows = first_ref.shape[1]
    numbers = lax.broadcasted_iota(jnp.int32, (tokens, rows), 1)
    numbers = (numbers - jnp.where((numbers & CAP) != 0, CAP, 0)).astype(jnp.float32)
    first = jnp.where(numbers == row_to_column(place_ref[0:1, :], tokens), 1.0, 0.0)
    second = jnp.where(numbers == row_to_column(place_ref[1:2, :], tokens), 1.0, 0.0)
    first_ref[...] = first.astype(jnp.bfloat16)
    second_ref[...] = second.astype(jnp.bfloat16)
    both_ref[...] = (first + second).astype(jnp.bfloat16)


def select(place):
    tokens = place.shape[1]
    shape = jax.ShapeDtypeStruct((tokens, tokens * CAP), jnp.bfloat16)
    return pl.pallas_call(select_kernel, out_shape=(shape,) * 3, name="select")(place)


def send_cot_kernel(cot_ref, pick_ref, weight_ref, out_ref):
    rows = jnp.dot(pick_ref[...], cot_ref[...], preferred_element_type=jnp.float32)
    rows = (rows * weight_ref[...]).astype(jnp.bfloat16).reshape(-1, CAP, cot_ref.shape[1])
    out_ref[:, 0] = rows
    out_ref[:, 1] = rows


def send_cot(cotangent, pick, slot_weight, steps=4):
    tokens, width = cotangent.shape
    experts = pick.shape[0] // CAP
    return pl.pallas_call(
        send_cot_kernel,
        grid=(steps,),
        in_specs=[
            pl.BlockSpec(cotangent.shape, lambda i: (0, 0)),
            pl.BlockSpec((experts * CAP // steps, tokens), lambda i: (i, 0)),
            pl.BlockSpec((experts * CAP // steps, 1), lambda i: (i, 0)),
        ],
        out_specs=pl.BlockSpec((experts // steps, 2, CAP, width), lambda i: (i, 0, 0, 0)),
        out_shape=jax.ShapeDtypeStruct((experts, 2, CAP, width), jnp.bfloat16),
        compiler_params=pltpu.CompilerParams(vmem_limit_bytes=VMEM_LIMIT),
        cost_estimate=pl.CostEstimate(flops=2 * experts * CAP * tokens * width, bytes_accessed=10_000_000, transcendentals=0),
        name="send_cot",
    )(cotangent, pick, slot_weight)


def finish_out_kernel(back_ref, first_ref, second_ref, weight_ref, cot_ref, out_ref, grad_ref):
    tokens, part = out_ref.shape
    rows = back_ref[...].reshape(-1, part)
    first = jnp.dot(first_ref[...], rows, preferred_element_type=jnp.float32)
    second = jnp.dot(second_ref[...], rows, preferred_element_type=jnp.float32)
    first = first.astype(jnp.bfloat16).astype(jnp.float32)
    second = second.astype(jnp.bfloat16).astype(jnp.float32)
    cot = cot_ref[...].astype(jnp.float32)
    total = first * row_to_column(weight_ref[0:1, :], tokens) + second * row_to_column(weight_ref[1:2, :], tokens)
    out_ref[...] = total.astype(jnp.bfloat16)

    @pl.when(pl.program_id(0) == 0)
    def _():
        grad_ref[...] = jnp.zeros_like(grad_ref)

    grad_ref[0:1, :] += column_to_row(jnp.sum(cot * first, axis=1, keepdims=True), tokens)
    grad_ref[1:2, :] += column_to_row(jnp.sum(cot * second, axis=1, keepdims=True), tokens)


def finish_out(back, first, second, weight, cotangent, steps=4):
    nodes, cap, width = back.shape
    tokens = cotangent.shape[0]
    part = width // steps
    whole = lambda i: (0, 0)
    return pl.pallas_call(
        finish_out_kernel,
        grid=(steps,),
        in_specs=[
            pl.BlockSpec((nodes, cap, part), lambda i: (0, 0, i)),
            pl.BlockSpec(first.shape, whole),
            pl.BlockSpec(second.shape, whole),
            pl.BlockSpec(weight.shape, whole),
            pl.BlockSpec((tokens, part), lambda i: (0, i)),
        ],
        out_specs=(
            pl.BlockSpec((tokens, part), lambda i: (0, i)),
            pl.BlockSpec((2, tokens), whole),
        ),
        out_shape=(
            jax.ShapeDtypeStruct((tokens, width), jnp.bfloat16),
            jax.ShapeDtypeStruct((2, tokens), jnp.float32),
        ),
        compiler_params=pltpu.CompilerParams(vmem_limit_bytes=VMEM_LIMIT),
        cost_estimate=pl.CostEstimate(flops=4 * nodes * cap * tokens * width, bytes_accessed=10_000_000, transcendentals=0),
        name="finish_out",
    )(back, first, second, weight, cotangent)


def finish_in_kernel(back_ref, both_ref, out_ref):
    rows = back_ref[...].reshape(-1, out_ref.shape[1])
    out_ref[...] = jnp.dot(both_ref[...], rows, preferred_element_type=jnp.float32).astype(jnp.bfloat16)


def finish_in(back, both, steps=4):
    nodes, cap, width = back.shape
    tokens = both.shape[0]
    part = width // steps
    return pl.pallas_call(
        finish_in_kernel,
        grid=(steps,),
        in_specs=[
            pl.BlockSpec((nodes, cap, part), lambda i: (0, 0, i)),
            pl.BlockSpec(both.shape, lambda i: (0, 0)),
        ],
        out_specs=pl.BlockSpec((tokens, part), lambda i: (0, i)),
        out_shape=jax.ShapeDtypeStruct((tokens, width), jnp.bfloat16),
        compiler_params=pltpu.CompilerParams(vmem_limit_bytes=VMEM_LIMIT),
        name="finish_in",
    )(back, both)


def dot(a, b, a_dim, b_dim):
    return lax.dot_general(a, b, (((a_dim,), (b_dim,)), ((), ())), preferred_element_type=jnp.float32)


def exchange(rows):
    return lax.all_to_all(rows, AXES, split_axis=0, concat_axis=0, tiled=True)


def on_device(coded, block_scale, routes, route_weight, cotangent, w_gate, w_up, w_down):
    tokens, width = coded.shape
    nodes = lax.axis_size(AXES)
    weight = route_weight.T
    gate_w, up_w, down_w = w_gate[0].T, w_up[0].T, w_down[0]

    send_rows, pick, slot_weight, place = prepare(coded, block_scale.T, routes.T, weight)
    rows = exchange(send_rows.reshape(nodes, CAP, width))
    cot_rows = exchange(send_cot(cotangent, pick, slot_weight).reshape(nodes, CAP, width))
    rows = rows.reshape(-1, width)
    cot_rows = cot_rows.reshape(-1, width)

    gate = dot(rows, gate_w, 1, 1)
    upper = dot(rows, up_w, 1, 1)
    sigma = jax.nn.sigmoid(gate)
    active = gate * sigma
    hidden = (active * upper).astype(jnp.bfloat16)
    partial_out = dot(hidden, down_w, 1, 0).astype(jnp.bfloat16)
    partial_out, cot_rows = lax.optimization_barrier((partial_out, cot_rows))
    back_out = exchange(partial_out.reshape(nodes, CAP, width))

    d_hidden = dot(cot_rows, down_w, 1, 1)
    d_upper = (d_hidden * active).astype(jnp.bfloat16)
    d_gate = (d_hidden * upper * sigma * (1.0 + gate * (1.0 - sigma))).astype(jnp.bfloat16)
    partial_in = (dot(d_gate, gate_w, 1, 0) + dot(d_upper, up_w, 1, 0)).astype(jnp.bfloat16)
    back_in = exchange(partial_in.reshape(nodes, CAP, width))

    grad_down = dot(hidden, cot_rows, 0, 0).astype(jnp.bfloat16)
    grad_gate = dot(d_gate, rows, 0, 0).astype(jnp.bfloat16)
    grad_up = dot(d_upper, rows, 0, 0).astype(jnp.bfloat16)

    first, second, both = select(place)
    layer_out, grad_weight = finish_out(back_out, first, second, weight, cotangent)
    grad_input = finish_in(back_in, both)
    return (layer_out, grad_input, grad_weight.T, grad_gate.T[None], grad_up.T[None], grad_down[None])


def solution(mesh):
    rows = P(AXES, None)
    matrix = P(AXES, None, None)
    return jax.shard_map(
        on_device,
        mesh=mesh,
        in_specs=(rows, rows, rows, rows, rows, matrix, matrix, matrix),
        out_specs=(rows, rows, rows, matrix, matrix, matrix),
        check_vma=False,
    )
```

```python
import jax
import jax.numpy as jnp
from jax import lax
from jax.experimental import pallas as pl
from jax.experimental.pallas import tpu as pltpu
from jax.sharding import PartitionSpec as P

AXES = ("dp", "expert")
CAP = 8
VMEM_LIMIT = 60 * 1024 * 1024


def row_to_column(row, size):
    eye = lax.broadcasted_iota(jnp.int32, (size, size), 0) == lax.broadcasted_iota(jnp.int32, (size, size), 1)
    return jnp.sum(jnp.where(eye, row, 0.0), axis=1, keepdims=True)


def column_to_row(column, size):
    eye = lax.broadcasted_iota(jnp.int32, (size, size), 0) == lax.broadcasted_iota(jnp.int32, (size, size), 1)
    return jnp.sum(jnp.where(eye, column, 0.0), axis=0, keepdims=True)


def prepare_kernel(coded_hbm, scale_ref, routes_ref, weight_ref, out_ref, pick_ref, slot_weight_ref, place_ref, coded_ref, inputs_ref, sem):
    tokens, width = coded_ref.shape
    blocks = scale_ref.shape[0]
    size = width // blocks
    experts = tokens // 2
    part = out_ref.shape[0] * CAP
    step = pl.program_id(0)

    @pl.when(step == 0)
    def _():
        copy = pltpu.make_async_copy(coded_hbm, coded_ref, sem)
        copy.start()
        numbers = lax.broadcasted_iota(jnp.int32, (experts, tokens), 0)
        first = routes_ref[0:1, :] == numbers
        second = routes_ref[1:2, :] == numbers
        named = jnp.where(first | second, 1.0, 0.0)
        earlier = lax.broadcasted_iota(jnp.int32, (tokens, tokens), 0) < lax.broadcasted_iota(jnp.int32, (tokens, tokens), 1)
        rank = jnp.dot(
            named.astype(jnp.bfloat16),
            jnp.where(earlier, 1.0, 0.0).astype(jnp.bfloat16),
            preferred_element_type=jnp.float32,
        )
        weight = jnp.where(first, weight_ref[0:1, :], 0.0) + jnp.where(second, weight_ref[1:2, :], 0.0)
        slots = lax.broadcasted_iota(jnp.int32, (experts, CAP, tokens), 1).astype(jnp.float32)
        slot_of = jnp.where(named > 0.0, rank, -1.0)
        pick = jnp.broadcast_to(slot_of[:, None, :], (experts, CAP, tokens)) == slots
        pick_ref[...] = jnp.where(pick, 1.0, 0.0).astype(jnp.bfloat16).reshape(experts * CAP, tokens)
        spread = jnp.broadcast_to(weight[:, None, :], (experts, CAP, tokens))
        slot_weight_ref[...] = jnp.sum(jnp.where(pick, spread, 0.0).reshape(experts * CAP, tokens), axis=1, keepdims=True)
        place = numbers.astype(jnp.float32) * (2 * CAP) + rank
        place_ref[0:1, :] = jnp.sum(jnp.where(first, place, 0.0), axis=0, keepdims=True)
        place_ref[1:2, :] = jnp.sum(jnp.where(second, place, 0.0), axis=0, keepdims=True)
        copy.wait()
        for b in range(blocks):
            columns = pl.ds(b * size, size)
            scale = row_to_column(scale_ref[b : b + 1, :], tokens)
            inputs_ref[:, columns] = (coded_ref[:, columns].astype(jnp.float32) * scale).astype(jnp.bfloat16)

    pick = pick_ref[pl.ds(pl.multiple_of(step * part, part), part), :]
    rows = jnp.dot(pick, inputs_ref[...], preferred_element_type=jnp.float32).astype(jnp.bfloat16)
    rows = rows.reshape(-1, CAP, width)
    out_ref[:, 0] = rows
    out_ref[:, 1] = rows


def prepare(coded, scale, routes, weight, steps=2):
    tokens, width = coded.shape
    experts = tokens // 2
    whole = lambda i: (0, 0)
    return pl.pallas_call(
        prepare_kernel,
        grid=(steps,),
        in_specs=[
            pl.BlockSpec(memory_space=pl.ANY),
            pl.BlockSpec(scale.shape, whole),
            pl.BlockSpec(routes.shape, whole),
            pl.BlockSpec(weight.shape, whole),
        ],
        out_specs=(
            pl.BlockSpec((experts // steps, 2, CAP, width), lambda i: (i, 0, 0, 0)),
            pl.BlockSpec((experts * CAP, tokens), whole),
            pl.BlockSpec((experts * CAP, 1), whole),
            pl.BlockSpec((2, tokens), whole),
        ),
        out_shape=(
            jax.ShapeDtypeStruct((experts, 2, CAP, width), jnp.bfloat16),
            jax.ShapeDtypeStruct((experts * CAP, tokens), jnp.bfloat16),
            jax.ShapeDtypeStruct((experts * CAP, 1), jnp.float32),
            jax.ShapeDtypeStruct((2, tokens), jnp.float32),
        ),
        scratch_shapes=[
            pltpu.VMEM((tokens, width), jnp.bfloat16),
            pltpu.VMEM((tokens, width), jnp.bfloat16),
            pltpu.SemaphoreType.DMA(()),
        ],
        compiler_params=pltpu.CompilerParams(vmem_limit_bytes=VMEM_LIMIT),
        name="prepare",
    )(coded, scale, routes, weight)


def select_kernel(place_ref, first_ref, second_ref, both_ref):
    tokens = place_ref.shape[1]
    rows = first_ref.shape[1]
    numbers = lax.broadcasted_iota(jnp.int32, (tokens, rows), 1)
    numbers = (numbers - jnp.where((numbers & CAP) != 0, CAP, 0)).astype(jnp.float32)
    first = jnp.where(numbers == row_to_column(place_ref[0:1, :], tokens), 1.0, 0.0)
    second = jnp.where(numbers == row_to_column(place_ref[1:2, :], tokens), 1.0, 0.0)
    first_ref[...] = first.astype(jnp.bfloat16)
    second_ref[...] = second.astype(jnp.bfloat16)
    both_ref[...] = (first + second).astype(jnp.bfloat16)


def select(place):
    tokens = place.shape[1]
    shape = jax.ShapeDtypeStruct((tokens, tokens * CAP), jnp.bfloat16)
    return pl.pallas_call(select_kernel, out_shape=(shape,) * 3, name="select")(place)


def send_cot_kernel(cot_ref, pick_ref, weight_ref, out_ref):
    rows = jnp.dot(pick_ref[...], cot_ref[...], preferred_element_type=jnp.float32)
    rows = (rows * weight_ref[...]).astype(jnp.bfloat16).reshape(-1, CAP, cot_ref.shape[1])
    out_ref[:, 0] = rows
    out_ref[:, 1] = rows


def send_cot(cotangent, pick, slot_weight, steps=4):
    tokens, width = cotangent.shape
    experts = pick.shape[0] // CAP
    return pl.pallas_call(
        send_cot_kernel,
        grid=(steps,),
        in_specs=[
            pl.BlockSpec(cotangent.shape, lambda i: (0, 0)),
            pl.BlockSpec((experts * CAP // steps, tokens), lambda i: (i, 0)),
            pl.BlockSpec((experts * CAP // steps, 1), lambda i: (i, 0)),
        ],
        out_specs=pl.BlockSpec((experts // steps, 2, CAP, width), lambda i: (i, 0, 0, 0)),
        out_shape=jax.ShapeDtypeStruct((experts, 2, CAP, width), jnp.bfloat16),
        compiler_params=pltpu.CompilerParams(vmem_limit_bytes=VMEM_LIMIT),
        cost_estimate=pl.CostEstimate(flops=2 * experts * CAP * tokens * width, bytes_accessed=10_000_000, transcendentals=0),
        name="send_cot",
    )(cotangent, pick, slot_weight)


def finish_out_kernel(back_ref, first_ref, second_ref, weight_ref, cot_ref, out_ref, grad_ref):
    tokens, part = out_ref.shape
    rows = back_ref[...].reshape(-1, part)
    first = jnp.dot(first_ref[...], rows, preferred_element_type=jnp.float32)
    second = jnp.dot(second_ref[...], rows, preferred_element_type=jnp.float32)
    first = first.astype(jnp.bfloat16).astype(jnp.float32)
    second = second.astype(jnp.bfloat16).astype(jnp.float32)
    cot = cot_ref[...].astype(jnp.float32)
    total = first * row_to_column(weight_ref[0:1, :], tokens) + second * row_to_column(weight_ref[1:2, :], tokens)
    out_ref[...] = total.astype(jnp.bfloat16)

    @pl.when(pl.program_id(0) == 0)
    def _():
        grad_ref[...] = jnp.zeros_like(grad_ref)

    grad_ref[0:1, :] += column_to_row(jnp.sum(cot * first, axis=1, keepdims=True), tokens)
    grad_ref[1:2, :] += column_to_row(jnp.sum(cot * second, axis=1, keepdims=True), tokens)


def finish_out(back, first, second, weight, cotangent, steps=4):
    nodes, cap, width = back.shape
    tokens = cotangent.shape[0]
    part = width // steps
    whole = lambda i: (0, 0)
    return pl.pallas_call(
        finish_out_kernel,
        grid=(steps,),
        in_specs=[
            pl.BlockSpec((nodes, cap, part), lambda i: (0, 0, i)),
            pl.BlockSpec(first.shape, whole),
            pl.BlockSpec(second.shape, whole),
            pl.BlockSpec(weight.shape, whole),
            pl.BlockSpec((tokens, part), lambda i: (0, i)),
        ],
        out_specs=(
            pl.BlockSpec((tokens, part), lambda i: (0, i)),
            pl.BlockSpec((2, tokens), whole),
        ),
        out_shape=(
            jax.ShapeDtypeStruct((tokens, width), jnp.bfloat16),
            jax.ShapeDtypeStruct((2, tokens), jnp.float32),
        ),
        compiler_params=pltpu.CompilerParams(vmem_limit_bytes=VMEM_LIMIT),
        cost_estimate=pl.CostEstimate(flops=4 * nodes * cap * tokens * width, bytes_accessed=10_000_000, transcendentals=0),
        name="finish_out",
    )(back, first, second, weight, cotangent)


def finish_in_kernel(back_ref, both_ref, out_ref):
    rows = back_ref[...].reshape(-1, out_ref.shape[1])
    out_ref[...] = jnp.dot(both_ref[...], rows, preferred_element_type=jnp.float32).astype(jnp.bfloat16)


def finish_in(back, both, steps=2):
    nodes, cap, width = back.shape
    tokens = both.shape[0]
    part = width // steps
    return pl.pallas_call(
        finish_in_kernel,
        grid=(steps,),
        in_specs=[
            pl.BlockSpec((nodes, cap, part), lambda i: (0, 0, i)),
            pl.BlockSpec(both.shape, lambda i: (0, 0)),
        ],
        out_specs=pl.BlockSpec((tokens, part), lambda i: (0, i)),
        out_shape=jax.ShapeDtypeStruct((tokens, width), jnp.bfloat16),
        compiler_params=pltpu.CompilerParams(vmem_limit_bytes=VMEM_LIMIT),
        name="finish_in",
    )(back, both)


def dot(a, b, a_dim, b_dim):
    return lax.dot_general(a, b, (((a_dim,), (b_dim,)), ((), ())), preferred_element_type=jnp.float32)


def exchange(rows):
    return lax.all_to_all(rows, AXES, split_axis=0, concat_axis=0, tiled=True)


def on_device(coded, block_scale, routes, route_weight, cotangent, w_gate, w_up, w_down):
    tokens, width = coded.shape
    nodes = lax.axis_size(AXES)
    weight = route_weight.T
    gate_w, up_w, down_w = w_gate[0].T, w_up[0].T, w_down[0]

    send_rows, pick, slot_weight, place = prepare(coded, block_scale.T, routes.T, weight)
    rows = exchange(send_rows.reshape(nodes, CAP, width))
    cot_rows = exchange(send_cot(cotangent, pick, slot_weight).reshape(nodes, CAP, width))
    rows = rows.reshape(-1, width)
    cot_rows = cot_rows.reshape(-1, width)

    gate = dot(rows, gate_w, 1, 1)
    upper = dot(rows, up_w, 1, 1)
    sigma = jax.nn.sigmoid(gate)
    active = gate * sigma
    hidden = (active * upper).astype(jnp.bfloat16)
    partial_out = dot(hidden, down_w, 1, 0).astype(jnp.bfloat16)
    partial_out, cot_rows = lax.optimization_barrier((partial_out, cot_rows))
    back_out = exchange(partial_out.reshape(nodes, CAP, width))

    d_hidden = dot(cot_rows, down_w, 1, 1)
    d_upper = (d_hidden * active).astype(jnp.bfloat16)
    d_gate = (d_hidden * upper * sigma * (1.0 + gate * (1.0 - sigma))).astype(jnp.bfloat16)
    partial_in = (dot(d_gate, gate_w, 1, 0) + dot(d_upper, up_w, 1, 0)).astype(jnp.bfloat16)
    partial_in, back_out = lax.optimization_barrier((partial_in, back_out))
    back_in = exchange(partial_in.reshape(nodes, CAP, width))

    grad_down = dot(hidden, cot_rows, 0, 0).astype(jnp.bfloat16)
    grad_gate = dot(d_gate, rows, 0, 0).astype(jnp.bfloat16)
    grad_up = dot(d_upper, rows, 0, 0).astype(jnp.bfloat16)

    first, second, both = select(place)
    layer_out, grad_weight = finish_out(back_out, first, second, weight, cotangent)
    grad_input = finish_in(back_in, both)
    return (layer_out, grad_input, grad_weight.T, grad_gate.T[None], grad_up.T[None], grad_down[None])


def solution(mesh):
    rows = P(AXES, None)
    matrix = P(AXES, None, None)
    return jax.shard_map(
        on_device,
        mesh=mesh,
        in_specs=(rows, rows, rows, rows, rows, matrix, matrix, matrix),
        out_specs=(rows, rows, rows, matrix, matrix, matrix),
        check_vma=False,
    )
```

```python
import jax
import jax.numpy as jnp
from jax import lax
from jax.experimental import pallas as pl
from jax.experimental.pallas import tpu as pltpu
from jax.sharding import PartitionSpec as P

AXES = ("dp", "expert")
CAP = 8
PARTS = 4
VMEM_LIMIT = 60 * 1024 * 1024


def row_to_column(row, size):
    eye = lax.broadcasted_iota(jnp.int32, (size, size), 0) == lax.broadcasted_iota(jnp.int32, (size, size), 1)
    return jnp.sum(jnp.where(eye, row, 0.0), axis=1, keepdims=True)


def column_to_row(column, size):
    eye = lax.broadcasted_iota(jnp.int32, (size, size), 0) == lax.broadcasted_iota(jnp.int32, (size, size), 1)
    return jnp.sum(jnp.where(eye, column, 0.0), axis=0, keepdims=True)


def pick_rows(routes_ref, experts, tokens):
    numbers = lax.broadcasted_iota(jnp.int32, (experts, tokens), 0)
    first = routes_ref[0:1, :] == numbers
    second = routes_ref[1:2, :] == numbers
    named = jnp.where(first | second, 1.0, 0.0)
    earlier = lax.broadcasted_iota(jnp.int32, (tokens, tokens), 0) < lax.broadcasted_iota(jnp.int32, (tokens, tokens), 1)
    rank = jnp.dot(
        named.astype(jnp.bfloat16),
        jnp.where(earlier, 1.0, 0.0).astype(jnp.bfloat16),
        preferred_element_type=jnp.float32,
    )
    slots = lax.broadcasted_iota(jnp.int32, (experts, CAP, tokens), 1).astype(jnp.float32)
    slot_of = jnp.where(named > 0.0, rank, -1.0)
    pick = jnp.broadcast_to(slot_of[:, None, :], (experts, CAP, tokens)) == slots
    return pick, first, second, rank


def as_matrix(pick):
    experts, cap, tokens = pick.shape
    return jnp.where(pick, 1.0, 0.0).astype(jnp.bfloat16).reshape(experts * cap, tokens)


def send_in_kernel(coded_hbm, scale_ref, routes_ref, out_hbm, coded_ref, rows_ref, in_sem, out_sem):
    tokens, width = coded_ref.shape
    blocks = scale_ref.shape[0]
    size = width // blocks
    part = width // PARTS
    experts = tokens // 2
    copies_in = []
    for k in range(PARTS):
        span = pl.ds(k * part, part)
        copies_in.append(pltpu.make_async_copy(coded_hbm.at[:, span], coded_ref.at[:, span], in_sem.at[k]))
        copies_in[k].start()
    pick = as_matrix(pick_rows(routes_ref, experts, tokens)[0])
    scales = [row_to_column(scale_ref[b : b + 1, :], tokens) for b in range(blocks)]
    copies = []
    for k in range(PARTS):
        span = pl.ds(k * part, part)
        copies_in[k].wait()
        for b in range(k * part // size, (k + 1) * part // size):
            columns = pl.ds(b * size, size)
            coded_ref[:, columns] = (coded_ref[:, columns].astype(jnp.float32) * scales[b]).astype(jnp.bfloat16)
        rows = jnp.dot(pick, coded_ref[:, span], preferred_element_type=jnp.float32)
        rows_ref[:, :, span] = rows.astype(jnp.bfloat16).reshape(experts, CAP, part)
        for half in range(2):
            copy = pltpu.make_async_copy(rows_ref.at[:, :, span], out_hbm.at[:, half, :, span], out_sem.at[k, half])
            copy.start()
            copies.append(copy)
    for copy in copies:
        copy.wait()


def send_in(coded, scale, routes):
    tokens, width = coded.shape
    experts = tokens // 2
    vmem = pl.BlockSpec(memory_space=pltpu.VMEM)
    hbm = pl.BlockSpec(memory_space=pl.ANY)
    return pl.pallas_call(
        send_in_kernel,
        in_specs=[hbm, vmem, vmem],
        out_specs=hbm,
        out_shape=jax.ShapeDtypeStruct((experts, 2, CAP, width), jnp.bfloat16),
        scratch_shapes=[
            pltpu.VMEM((tokens, width), jnp.bfloat16),
            pltpu.VMEM((experts, CAP, width), jnp.bfloat16),
            pltpu.SemaphoreType.DMA((PARTS,)),
            pltpu.SemaphoreType.DMA((PARTS, 2)),
        ],
        compiler_params=pltpu.CompilerParams(vmem_limit_bytes=VMEM_LIMIT),
        name="send_in",
    )(coded, scale, routes)


def plan_kernel(routes_ref, weight_ref, pick_ref, slot_weight_ref, place_ref):
    tokens = routes_ref.shape[1]
    experts = tokens // 2
    pick, first, second, rank = pick_rows(routes_ref, experts, tokens)
    pick_ref[...] = as_matrix(pick)
    weight = jnp.where(first, weight_ref[0:1, :], 0.0) + jnp.where(second, weight_ref[1:2, :], 0.0)
    spread = jnp.broadcast_to(weight[:, None, :], pick.shape)
    slot_weight_ref[...] = jnp.sum(jnp.where(pick, spread, 0.0).reshape(experts * CAP, tokens), axis=1, keepdims=True)
    place = lax.broadcasted_iota(jnp.int32, (experts, tokens), 0).astype(jnp.float32) * (2 * CAP) + rank
    place_ref[0:1, :] = jnp.sum(jnp.where(first, place, 0.0), axis=0, keepdims=True)
    place_ref[1:2, :] = jnp.sum(jnp.where(second, place, 0.0), axis=0, keepdims=True)


def plan(routes, weight):
    tokens = routes.shape[1]
    experts = tokens // 2
    return pl.pallas_call(
        plan_kernel,
        out_shape=(
            jax.ShapeDtypeStruct((experts * CAP, tokens), jnp.bfloat16),
            jax.ShapeDtypeStruct((experts * CAP, 1), jnp.float32),
            jax.ShapeDtypeStruct((2, tokens), jnp.float32),
        ),
        compiler_params=pltpu.CompilerParams(vmem_limit_bytes=VMEM_LIMIT),
        name="plan",
    )(routes, weight)


def select_kernel(place_ref, first_ref, second_ref, both_ref):
    tokens = place_ref.shape[1]
    rows = first_ref.shape[1]
    numbers = lax.broadcasted_iota(jnp.int32, (tokens, rows), 1)
    numbers = (numbers - jnp.where((numbers & CAP) != 0, CAP, 0)).astype(jnp.float32)
    first = jnp.where(numbers == row_to_column(place_ref[0:1, :], tokens), 1.0, 0.0)
    second = jnp.where(numbers == row_to_column(place_ref[1:2, :], tokens), 1.0, 0.0)
    first_ref[...] = first.astype(jnp.bfloat16)
    second_ref[...] = second.astype(jnp.bfloat16)
    both_ref[...] = (first + second).astype(jnp.bfloat16)


def select(place):
    tokens = place.shape[1]
    shape = jax.ShapeDtypeStruct((tokens, tokens * CAP), jnp.bfloat16)
    return pl.pallas_call(select_kernel, out_shape=(shape,) * 3, name="select")(place)


def send_cot_kernel(cot_ref, pick_ref, weight_ref, out_ref):
    rows = jnp.dot(pick_ref[...], cot_ref[...], preferred_element_type=jnp.float32)
    rows = (rows * weight_ref[...]).astype(jnp.bfloat16).reshape(-1, CAP, cot_ref.shape[1])
    out_ref[:, 0] = rows
    out_ref[:, 1] = rows


def send_cot(cotangent, pick, slot_weight, steps=4):
    tokens, width = cotangent.shape
    experts = pick.shape[0] // CAP
    return pl.pallas_call(
        send_cot_kernel,
        grid=(steps,),
        in_specs=[
            pl.BlockSpec(cotangent.shape, lambda i: (0, 0)),
            pl.BlockSpec((experts * CAP // steps, tokens), lambda i: (i, 0)),
            pl.BlockSpec((experts * CAP // steps, 1), lambda i: (i, 0)),
        ],
        out_specs=pl.BlockSpec((experts // steps, 2, CAP, width), lambda i: (i, 0, 0, 0)),
        out_shape=jax.ShapeDtypeStruct((experts, 2, CAP, width), jnp.bfloat16),
        compiler_params=pltpu.CompilerParams(vmem_limit_bytes=VMEM_LIMIT),
        cost_estimate=pl.CostEstimate(flops=2 * experts * CAP * tokens * width, bytes_accessed=10_000_000, transcendentals=0),
        name="send_cot",
    )(cotangent, pick, slot_weight)


def finish_out_kernel(back_ref, first_ref, second_ref, weight_ref, cot_ref, out_ref, grad_ref):
    tokens, part = out_ref.shape
    rows = back_ref[...].reshape(-1, part)
    first = jnp.dot(first_ref[...], rows, preferred_element_type=jnp.float32)
    second = jnp.dot(second_ref[...], rows, preferred_element_type=jnp.float32)
    first = first.astype(jnp.bfloat16).astype(jnp.float32)
    second = second.astype(jnp.bfloat16).astype(jnp.float32)
    cot = cot_ref[...].astype(jnp.float32)
    total = first * row_to_column(weight_ref[0:1, :], tokens) + second * row_to_column(weight_ref[1:2, :], tokens)
    out_ref[...] = total.astype(jnp.bfloat16)

    @pl.when(pl.program_id(0) == 0)
    def _():
        grad_ref[...] = jnp.zeros_like(grad_ref)

    grad_ref[0:1, :] += column_to_row(jnp.sum(cot * first, axis=1, keepdims=True), tokens)
    grad_ref[1:2, :] += column_to_row(jnp.sum(cot * second, axis=1, keepdims=True), tokens)


def finish_out(back, first, second, weight, cotangent, steps=4):
    nodes, cap, width = back.shape
    tokens = cotangent.shape[0]
    part = width // steps
    whole = lambda i: (0, 0)
    return pl.pallas_call(
        finish_out_kernel,
        grid=(steps,),
        in_specs=[
            pl.BlockSpec((nodes, cap, part), lambda i: (0, 0, i)),
            pl.BlockSpec(first.shape, whole),
            pl.BlockSpec(second.shape, whole),
            pl.BlockSpec(weight.shape, whole),
            pl.BlockSpec((tokens, part), lambda i: (0, i)),
        ],
        out_specs=(
            pl.BlockSpec((tokens, part), lambda i: (0, i)),
            pl.BlockSpec((2, tokens), whole),
        ),
        out_shape=(
            jax.ShapeDtypeStruct((tokens, width), jnp.bfloat16),
            jax.ShapeDtypeStruct((2, tokens), jnp.float32),
        ),
        compiler_params=pltpu.CompilerParams(vmem_limit_bytes=VMEM_LIMIT),
        cost_estimate=pl.CostEstimate(flops=4 * nodes * cap * tokens * width, bytes_accessed=10_000_000, transcendentals=0),
        name="finish_out",
    )(back, first, second, weight, cotangent)


def finish_in_kernel(back_ref, both_ref, out_ref):
    rows = back_ref[...].reshape(-1, out_ref.shape[1])
    out_ref[...] = jnp.dot(both_ref[...], rows, preferred_element_type=jnp.float32).astype(jnp.bfloat16)


def finish_in(back, both, steps=2):
    nodes, cap, width = back.shape
    tokens = both.shape[0]
    part = width // steps
    return pl.pallas_call(
        finish_in_kernel,
        grid=(steps,),
        in_specs=[
            pl.BlockSpec((nodes, cap, part), lambda i: (0, 0, i)),
            pl.BlockSpec(both.shape, lambda i: (0, 0)),
        ],
        out_specs=pl.BlockSpec((tokens, part), lambda i: (0, i)),
        out_shape=jax.ShapeDtypeStruct((tokens, width), jnp.bfloat16),
        compiler_params=pltpu.CompilerParams(vmem_limit_bytes=VMEM_LIMIT),
        name="finish_in",
    )(back, both)


def dot(a, b, a_dim, b_dim):
    return lax.dot_general(a, b, (((a_dim,), (b_dim,)), ((), ())), preferred_element_type=jnp.float32)


def exchange(rows):
    return lax.all_to_all(rows, AXES, split_axis=0, concat_axis=0, tiled=True)


def on_device(coded, block_scale, routes, route_weight, cotangent, w_gate, w_up, w_down):
    tokens, width = coded.shape
    nodes = lax.axis_size(AXES)
    weight = route_weight.T
    gate_w, up_w, down_w = w_gate[0].T, w_up[0].T, w_down[0]

    send_rows = send_in(coded, block_scale.T, routes.T)
    rows = exchange(send_rows.reshape(nodes, CAP, width))
    late_routes, _ = lax.optimization_barrier((routes.T, send_rows))
    pick, slot_weight, place = plan(late_routes, weight)
    rows, send_cots = lax.optimization_barrier((rows, send_cot(cotangent, pick, slot_weight)))
    cot_rows = exchange(send_cots.reshape(nodes, CAP, width))
    rows = rows.reshape(-1, width)
    cot_rows = cot_rows.reshape(-1, width)

    gate = dot(rows, gate_w, 1, 1)
    upper = dot(rows, up_w, 1, 1)
    sigma = jax.nn.sigmoid(gate)
    active = gate * sigma
    hidden = (active * upper).astype(jnp.bfloat16)
    partial_out = dot(hidden, down_w, 1, 0).astype(jnp.bfloat16)
    partial_out, cot_rows = lax.optimization_barrier((partial_out, cot_rows))
    back_out = exchange(partial_out.reshape(nodes, CAP, width))

    d_hidden = dot(cot_rows, down_w, 1, 1)
    d_upper = (d_hidden * active).astype(jnp.bfloat16)
    d_gate = (d_hidden * upper * sigma * (1.0 + gate * (1.0 - sigma))).astype(jnp.bfloat16)
    partial_in = (dot(d_gate, gate_w, 1, 0) + dot(d_upper, up_w, 1, 0)).astype(jnp.bfloat16)
    partial_in, back_out = lax.optimization_barrier((partial_in, back_out))
    back_in = exchange(partial_in.reshape(nodes, CAP, width))

    grad_down = dot(hidden, cot_rows, 0, 0).astype(jnp.bfloat16)
    grad_gate = dot(d_gate, rows, 0, 0).astype(jnp.bfloat16)
    grad_up = dot(d_upper, rows, 0, 0).astype(jnp.bfloat16)

    first, second, both = select(place)
    layer_out, grad_weight = finish_out(back_out, first, second, weight, cotangent)
    grad_input = finish_in(back_in, both)
    return (layer_out, grad_input, grad_weight.T, grad_gate.T[None], grad_up.T[None], grad_down[None])


def solution(mesh):
    rows = P(AXES, None)
    matrix = P(AXES, None, None)
    return jax.shard_map(
        on_device,
        mesh=mesh,
        in_specs=(rows, rows, rows, rows, rows, matrix, matrix, matrix),
        out_specs=(rows, rows, rows, matrix, matrix, matrix),
        check_vma=False,
    )
```

```python
import jax
import jax.numpy as jnp
from jax import lax
from jax.experimental import pallas as pl
from jax.experimental.pallas import tpu as pltpu
from jax.sharding import PartitionSpec as P

AXES = ("dp", "expert")
CAP = 8
PARTS = 4
VMEM_LIMIT = 60 * 1024 * 1024


def row_to_column(row, size):
    eye = lax.broadcasted_iota(jnp.int32, (size, size), 0) == lax.broadcasted_iota(jnp.int32, (size, size), 1)
    return jnp.sum(jnp.where(eye, row, 0.0), axis=1, keepdims=True)


def column_to_row(column, size):
    eye = lax.broadcasted_iota(jnp.int32, (size, size), 0) == lax.broadcasted_iota(jnp.int32, (size, size), 1)
    return jnp.sum(jnp.where(eye, column, 0.0), axis=0, keepdims=True)


def pick_rows(routes_ref, experts, tokens):
    numbers = lax.broadcasted_iota(jnp.int32, (experts, tokens), 0)
    first = routes_ref[0:1, :] == numbers
    second = routes_ref[1:2, :] == numbers
    named = jnp.where(first | second, 1.0, 0.0)
    earlier = lax.broadcasted_iota(jnp.int32, (tokens, tokens), 0) < lax.broadcasted_iota(jnp.int32, (tokens, tokens), 1)
    rank = jnp.dot(
        named.astype(jnp.bfloat16),
        jnp.where(earlier, 1.0, 0.0).astype(jnp.bfloat16),
        preferred_element_type=jnp.float32,
    )
    slots = lax.broadcasted_iota(jnp.int32, (experts, CAP, tokens), 1).astype(jnp.float32)
    slot_of = jnp.where(named > 0.0, rank, -1.0)
    pick = jnp.broadcast_to(slot_of[:, None, :], (experts, CAP, tokens)) == slots
    return pick, first, second, rank


def as_matrix(pick):
    experts, cap, tokens = pick.shape
    return jnp.where(pick, 1.0, 0.0).astype(jnp.bfloat16).reshape(experts * cap, tokens)


def send_in_kernel(coded_hbm, scale_hbm, routes_hbm, out_hbm, coded_ref, rows_ref, scale_ref, routes_ref, in_sem, out_sem):
    tokens, width = coded_ref.shape
    blocks = scale_ref.shape[0]
    size = width // blocks
    part = width // PARTS
    experts = tokens // 2
    copy_routes = pltpu.make_async_copy(routes_hbm, routes_ref, in_sem.at[0])
    copy_routes.start()
    copy_scale = pltpu.make_async_copy(scale_hbm, scale_ref, in_sem.at[1])
    copy_scale.start()
    copy_coded = pltpu.make_async_copy(coded_hbm, coded_ref, in_sem.at[2])
    copy_coded.start()
    copy_routes.wait()
    pick = as_matrix(pick_rows(routes_ref, experts, tokens)[0])
    copy_scale.wait()
    scales = [row_to_column(scale_ref[b : b + 1, :], tokens) for b in range(blocks)]
    copy_coded.wait()
    copies = []
    for k in range(PARTS):
        span = pl.ds(k * part, part)
        for b in range(k * part // size, (k + 1) * part // size):
            columns = pl.ds(b * size, size)
            coded_ref[:, columns] = (coded_ref[:, columns].astype(jnp.float32) * scales[b]).astype(jnp.bfloat16)
        rows = jnp.dot(pick, coded_ref[:, span], preferred_element_type=jnp.float32)
        rows_ref[:, :, span] = rows.astype(jnp.bfloat16).reshape(experts, CAP, part)
        for half in range(2):
            copy = pltpu.make_async_copy(rows_ref.at[:, :, span], out_hbm.at[:, half, :, span], out_sem.at[k, half])
            copy.start()
            copies.append(copy)
    for copy in copies:
        copy.wait()


def send_in(coded, scale, routes):
    tokens, width = coded.shape
    experts = tokens // 2
    hbm = pl.BlockSpec(memory_space=pl.ANY)
    return pl.pallas_call(
        send_in_kernel,
        in_specs=[hbm, hbm, hbm],
        out_specs=hbm,
        out_shape=jax.ShapeDtypeStruct((experts, 2, CAP, width), jnp.bfloat16),
        scratch_shapes=[
            pltpu.VMEM((tokens, width), jnp.bfloat16),
            pltpu.VMEM((experts, CAP, width), jnp.bfloat16),
            pltpu.VMEM(scale.shape, jnp.float32),
            pltpu.VMEM(routes.shape, jnp.int32),
            pltpu.SemaphoreType.DMA((3,)),
            pltpu.SemaphoreType.DMA((PARTS, 2)),
        ],
        compiler_params=pltpu.CompilerParams(vmem_limit_bytes=VMEM_LIMIT),
        name="send_in",
    )(coded, scale, routes)


def plan_kernel(routes_ref, weight_ref, pick_ref, slot_weight_ref, place_ref):
    tokens = routes_ref.shape[1]
    experts = tokens // 2
    pick, first, second, rank = pick_rows(routes_ref, experts, tokens)
    pick_ref[...] = as_matrix(pick)
    weight = jnp.where(first, weight_ref[0:1, :], 0.0) + jnp.where(second, weight_ref[1:2, :], 0.0)
    spread = jnp.broadcast_to(weight[:, None, :], pick.shape)
    slot_weight_ref[...] = jnp.sum(jnp.where(pick, spread, 0.0).reshape(experts * CAP, tokens), axis=1, keepdims=True)
    place = lax.broadcasted_iota(jnp.int32, (experts, tokens), 0).astype(jnp.float32) * (2 * CAP) + rank
    place_ref[0:1, :] = jnp.sum(jnp.where(first, place, 0.0), axis=0, keepdims=True)
    place_ref[1:2, :] = jnp.sum(jnp.where(second, place, 0.0), axis=0, keepdims=True)


def plan(routes, weight):
    tokens = routes.shape[1]
    experts = tokens // 2
    return pl.pallas_call(
        plan_kernel,
        out_shape=(
            jax.ShapeDtypeStruct((experts * CAP, tokens), jnp.bfloat16),
            jax.ShapeDtypeStruct((experts * CAP, 1), jnp.float32),
            jax.ShapeDtypeStruct((2, tokens), jnp.float32),
        ),
        compiler_params=pltpu.CompilerParams(vmem_limit_bytes=VMEM_LIMIT),
        name="plan",
    )(routes, weight)


def select_kernel(place_ref, first_ref, second_ref, both_ref):
    tokens = place_ref.shape[1]
    rows = first_ref.shape[1]
    numbers = lax.broadcasted_iota(jnp.int32, (tokens, rows), 1)
    numbers = (numbers - jnp.where((numbers & CAP) != 0, CAP, 0)).astype(jnp.float32)
    first = jnp.where(numbers == row_to_column(place_ref[0:1, :], tokens), 1.0, 0.0)
    second = jnp.where(numbers == row_to_column(place_ref[1:2, :], tokens), 1.0, 0.0)
    first_ref[...] = first.astype(jnp.bfloat16)
    second_ref[...] = second.astype(jnp.bfloat16)
    both_ref[...] = (first + second).astype(jnp.bfloat16)


def select(place):
    tokens = place.shape[1]
    shape = jax.ShapeDtypeStruct((tokens, tokens * CAP), jnp.bfloat16)
    return pl.pallas_call(select_kernel, out_shape=(shape,) * 3, name="select")(place)


def send_cot_kernel(cot_ref, pick_ref, weight_ref, out_ref):
    rows = jnp.dot(pick_ref[...], cot_ref[...], preferred_element_type=jnp.float32)
    rows = (rows * weight_ref[...]).astype(jnp.bfloat16).reshape(-1, CAP, cot_ref.shape[1])
    out_ref[:, 0] = rows
    out_ref[:, 1] = rows


def send_cot(cotangent, pick, slot_weight, steps=4):
    tokens, width = cotangent.shape
    experts = pick.shape[0] // CAP
    return pl.pallas_call(
        send_cot_kernel,
        grid=(steps,),
        in_specs=[
            pl.BlockSpec(cotangent.shape, lambda i: (0, 0)),
            pl.BlockSpec((experts * CAP // steps, tokens), lambda i: (i, 0)),
            pl.BlockSpec((experts * CAP // steps, 1), lambda i: (i, 0)),
        ],
        out_specs=pl.BlockSpec((experts // steps, 2, CAP, width), lambda i: (i, 0, 0, 0)),
        out_shape=jax.ShapeDtypeStruct((experts, 2, CAP, width), jnp.bfloat16),
        compiler_params=pltpu.CompilerParams(vmem_limit_bytes=VMEM_LIMIT),
        cost_estimate=pl.CostEstimate(flops=2 * experts * CAP * tokens * width, bytes_accessed=10_000_000, transcendentals=0),
        name="send_cot",
    )(cotangent, pick, slot_weight)


def finish_out_kernel(back_ref, first_ref, second_ref, weight_ref, cot_ref, out_ref, grad_ref):
    tokens, part = out_ref.shape
    rows = back_ref[...].reshape(-1, part)
    first = jnp.dot(first_ref[...], rows, preferred_element_type=jnp.float32)
    second = jnp.dot(second_ref[...], rows, preferred_element_type=jnp.float32)
    first = first.astype(jnp.bfloat16).astype(jnp.float32)
    second = second.astype(jnp.bfloat16).astype(jnp.float32)
    cot = cot_ref[...].astype(jnp.float32)
    total = first * row_to_column(weight_ref[0:1, :], tokens) + second * row_to_column(weight_ref[1:2, :], tokens)
    out_ref[...] = total.astype(jnp.bfloat16)

    @pl.when(pl.program_id(0) == 0)
    def _():
        grad_ref[...] = jnp.zeros_like(grad_ref)

    grad_ref[0:1, :] += column_to_row(jnp.sum(cot * first, axis=1, keepdims=True), tokens)
    grad_ref[1:2, :] += column_to_row(jnp.sum(cot * second, axis=1, keepdims=True), tokens)


def finish_out(back, first, second, weight, cotangent, steps=4):
    nodes, cap, width = back.shape
    tokens = cotangent.shape[0]
    part = width // steps
    whole = lambda i: (0, 0)
    return pl.pallas_call(
        finish_out_kernel,
        grid=(steps,),
        in_specs=[
            pl.BlockSpec((nodes, cap, part), lambda i: (0, 0, i)),
            pl.BlockSpec(first.shape, whole),
            pl.BlockSpec(second.shape, whole),
            pl.BlockSpec(weight.shape, whole),
            pl.BlockSpec((tokens, part), lambda i: (0, i)),
        ],
        out_specs=(
            pl.BlockSpec((tokens, part), lambda i: (0, i)),
            pl.BlockSpec((2, tokens), whole),
        ),
        out_shape=(
            jax.ShapeDtypeStruct((tokens, width), jnp.bfloat16),
            jax.ShapeDtypeStruct((2, tokens), jnp.float32),
        ),
        compiler_params=pltpu.CompilerParams(vmem_limit_bytes=VMEM_LIMIT),
        cost_estimate=pl.CostEstimate(flops=4 * nodes * cap * tokens * width, bytes_accessed=10_000_000, transcendentals=0),
        name="finish_out",
    )(back, first, second, weight, cotangent)


def finish_in_kernel(back_ref, both_ref, out_ref):
    rows = back_ref[...].reshape(-1, out_ref.shape[1])
    out_ref[...] = jnp.dot(both_ref[...], rows, preferred_element_type=jnp.float32).astype(jnp.bfloat16)


def finish_in(back, both, steps=2):
    nodes, cap, width = back.shape
    tokens = both.shape[0]
    part = width // steps
    return pl.pallas_call(
        finish_in_kernel,
        grid=(steps,),
        in_specs=[
            pl.BlockSpec((nodes, cap, part), lambda i: (0, 0, i)),
            pl.BlockSpec(both.shape, lambda i: (0, 0)),
        ],
        out_specs=pl.BlockSpec((tokens, part), lambda i: (0, i)),
        out_shape=jax.ShapeDtypeStruct((tokens, width), jnp.bfloat16),
        compiler_params=pltpu.CompilerParams(vmem_limit_bytes=VMEM_LIMIT),
        name="finish_in",
    )(back, both)


def dot(a, b, a_dim, b_dim):
    return lax.dot_general(a, b, (((a_dim,), (b_dim,)), ((), ())), preferred_element_type=jnp.float32)


def exchange(rows):
    return lax.all_to_all(rows, AXES, split_axis=0, concat_axis=0, tiled=True)


def on_device(coded, block_scale, routes, route_weight, cotangent, w_gate, w_up, w_down):
    tokens, width = coded.shape
    nodes = lax.axis_size(AXES)
    weight = route_weight.T
    gate_w, up_w, down_w = w_gate[0].T, w_up[0].T, w_down[0]

    send_rows = send_in(coded, block_scale.T, routes.T)
    rows = exchange(send_rows.reshape(nodes, CAP, width))
    late_routes, _ = lax.optimization_barrier((routes.T, send_rows))
    pick, slot_weight, place = plan(late_routes, weight)
    rows, send_cots = lax.optimization_barrier((rows, send_cot(cotangent, pick, slot_weight)))
    cot_rows = exchange(send_cots.reshape(nodes, CAP, width))
    rows = rows.reshape(-1, width)
    cot_rows = cot_rows.reshape(-1, width)

    gate = dot(rows, gate_w, 1, 1)
    upper = dot(rows, up_w, 1, 1)
    sigma = jax.nn.sigmoid(gate)
    active = gate * sigma
    hidden = (active * upper).astype(jnp.bfloat16)
    partial_out = dot(hidden, down_w, 1, 0).astype(jnp.bfloat16)
    partial_out, cot_rows = lax.optimization_barrier((partial_out, cot_rows))
    back_out = exchange(partial_out.reshape(nodes, CAP, width))

    d_hidden = dot(cot_rows, down_w, 1, 1)
    d_upper = (d_hidden * active).astype(jnp.bfloat16)
    d_gate = (d_hidden * upper * sigma * (1.0 + gate * (1.0 - sigma))).astype(jnp.bfloat16)
    partial_in = (dot(d_gate, gate_w, 1, 0) + dot(d_upper, up_w, 1, 0)).astype(jnp.bfloat16)
    partial_in, back_out = lax.optimization_barrier((partial_in, back_out))
    back_in = exchange(partial_in.reshape(nodes, CAP, width))

    grad_down = dot(hidden, cot_rows, 0, 0).astype(jnp.bfloat16)
    grad_gate = dot(d_gate, rows, 0, 0).astype(jnp.bfloat16)
    grad_up = dot(d_upper, rows, 0, 0).astype(jnp.bfloat16)

    first, second, both = select(place)
    layer_out, grad_weight = finish_out(back_out, first, second, weight, cotangent)
    grad_input = finish_in(back_in, both)
    return (layer_out, grad_input, grad_weight.T, grad_gate.T[None], grad_up.T[None], grad_down[None])


def solution(mesh):
    rows = P(AXES, None)
    matrix = P(AXES, None, None)
    return jax.shard_map(
        on_device,
        mesh=mesh,
        in_specs=(rows, rows, rows, rows, rows, matrix, matrix, matrix),
        out_specs=(rows, rows, rows, matrix, matrix, matrix),
        check_vma=False,
    )
```

```python
import jax
import jax.numpy as jnp
from jax import lax
from jax.experimental import pallas as pl
from jax.experimental.pallas import tpu as pltpu
from jax.sharding import PartitionSpec as P

AXES = ("dp", "expert")
CAP = 8
PARTS = 4
VMEM_LIMIT = 60 * 1024 * 1024


def row_to_column(row, size):
    eye = lax.broadcasted_iota(jnp.int32, (size, size), 0) == lax.broadcasted_iota(jnp.int32, (size, size), 1)
    return jnp.sum(jnp.where(eye, row, 0.0), axis=1, keepdims=True)


def column_to_row(column, size):
    eye = lax.broadcasted_iota(jnp.int32, (size, size), 0) == lax.broadcasted_iota(jnp.int32, (size, size), 1)
    return jnp.sum(jnp.where(eye, column, 0.0), axis=0, keepdims=True)


def pick_rows(routes_ref, experts, tokens):
    numbers = lax.broadcasted_iota(jnp.int32, (experts, tokens), 0)
    first = routes_ref[0:1, :] == numbers
    second = routes_ref[1:2, :] == numbers
    named = jnp.where(first | second, 1.0, 0.0)
    earlier = lax.broadcasted_iota(jnp.int32, (tokens, tokens), 0) < lax.broadcasted_iota(jnp.int32, (tokens, tokens), 1)
    rank = jnp.dot(
        named.astype(jnp.bfloat16),
        jnp.where(earlier, 1.0, 0.0).astype(jnp.bfloat16),
        preferred_element_type=jnp.float32,
    )
    slots = lax.broadcasted_iota(jnp.int32, (experts, CAP, tokens), 1).astype(jnp.float32)
    slot_of = jnp.where(named > 0.0, rank, -1.0)
    pick = jnp.broadcast_to(slot_of[:, None, :], (experts, CAP, tokens)) == slots
    return pick, first, second, rank


def as_matrix(pick):
    experts, cap, tokens = pick.shape
    return jnp.where(pick, 1.0, 0.0).astype(jnp.bfloat16).reshape(experts * cap, tokens)


def send_in_kernel(coded_hbm, scale_hbm, routes_hbm, out_hbm, coded_ref, rows_ref, scale_ref, routes_ref, in_sem, out_sem):
    tokens, width = coded_ref.shape
    blocks = scale_ref.shape[0]
    size = width // blocks
    part = width // PARTS
    experts = tokens // 2
    copy_routes = pltpu.make_async_copy(routes_hbm, routes_ref, in_sem.at[0])
    copy_routes.start()
    copy_scale = pltpu.make_async_copy(scale_hbm, scale_ref, in_sem.at[1])
    copy_scale.start()
    copy_coded = pltpu.make_async_copy(coded_hbm, coded_ref, in_sem.at[2])
    copy_coded.start()
    copy_routes.wait()
    pick = as_matrix(pick_rows(routes_ref, experts, tokens)[0])
    copy_scale.wait()
    scales = [row_to_column(scale_ref[b : b + 1, :], tokens) for b in range(blocks)]
    copy_coded.wait()
    copies = []
    for k in range(PARTS):
        span = pl.ds(k * part, part)
        for b in range(k * part // size, (k + 1) * part // size):
            columns = pl.ds(b * size, size)
            coded_ref[:, columns] = (coded_ref[:, columns].astype(jnp.float32) * scales[b]).astype(jnp.bfloat16)
        rows = jnp.dot(pick, coded_ref[:, span], preferred_element_type=jnp.float32)
        rows_ref[:, :, span] = rows.astype(jnp.bfloat16).reshape(experts, CAP, part)
        for half in range(2):
            copy = pltpu.make_async_copy(rows_ref.at[:, :, span], out_hbm.at[:, half, :, span], out_sem.at[k, half])
            copy.start()
            copies.append(copy)
    for copy in copies:
        copy.wait()


def send_in(coded, scale, routes):
    tokens, width = coded.shape
    experts = tokens // 2
    hbm = pl.BlockSpec(memory_space=pl.ANY)
    return pl.pallas_call(
        send_in_kernel,
        in_specs=[hbm, hbm, hbm],
        out_specs=hbm,
        out_shape=jax.ShapeDtypeStruct((experts, 2, CAP, width), jnp.bfloat16),
        scratch_shapes=[
            pltpu.VMEM((tokens, width), jnp.bfloat16),
            pltpu.VMEM((experts, CAP, width), jnp.bfloat16),
            pltpu.VMEM(scale.shape, jnp.float32),
            pltpu.VMEM(routes.shape, jnp.int32),
            pltpu.SemaphoreType.DMA((3,)),
            pltpu.SemaphoreType.DMA((PARTS, 2)),
        ],
        compiler_params=pltpu.CompilerParams(vmem_limit_bytes=VMEM_LIMIT),
        name="send_in",
    )(coded, scale, routes)


def plan_kernel(routes_ref, weight_ref, pick_ref, slot_weight_ref, place_ref):
    tokens = routes_ref.shape[1]
    experts = tokens // 2
    pick, first, second, rank = pick_rows(routes_ref, experts, tokens)
    pick_ref[...] = as_matrix(pick)
    weight = jnp.where(first, weight_ref[0:1, :], 0.0) + jnp.where(second, weight_ref[1:2, :], 0.0)
    spread = jnp.broadcast_to(weight[:, None, :], pick.shape)
    slot_weight_ref[...] = jnp.sum(jnp.where(pick, spread, 0.0).reshape(experts * CAP, tokens), axis=1, keepdims=True)
    place = lax.broadcasted_iota(jnp.int32, (experts, tokens), 0).astype(jnp.float32) * (2 * CAP) + rank
    place_ref[0:1, :] = jnp.sum(jnp.where(first, place, 0.0), axis=0, keepdims=True)
    place_ref[1:2, :] = jnp.sum(jnp.where(second, place, 0.0), axis=0, keepdims=True)


def plan(routes, weight):
    tokens = routes.shape[1]
    experts = tokens // 2
    return pl.pallas_call(
        plan_kernel,
        out_shape=(
            jax.ShapeDtypeStruct((experts * CAP, tokens), jnp.bfloat16),
            jax.ShapeDtypeStruct((experts * CAP, 1), jnp.float32),
            jax.ShapeDtypeStruct((2, tokens), jnp.float32),
        ),
        compiler_params=pltpu.CompilerParams(vmem_limit_bytes=VMEM_LIMIT),
        name="plan",
    )(routes, weight)


def select_kernel(place_ref, first_ref, second_ref, both_ref):
    tokens = place_ref.shape[1]
    rows = first_ref.shape[1]
    places = [row_to_column(place_ref[j : j + 1, :], tokens) for j in range(2)]
    numbers = lax.broadcasted_iota(jnp.int32, (tokens, rows), 1)
    numbers = (numbers - jnp.where((numbers & CAP) != 0, CAP, 0)).astype(jnp.float32)
    first_ref[...] = jnp.where(numbers == places[0], 1.0, 0.0).astype(jnp.bfloat16)
    second_ref[...] = jnp.where(numbers == places[1], 1.0, 0.0).astype(jnp.bfloat16)
    slots = lax.broadcasted_iota(jnp.int32, (tokens, rows // 2), 1)
    slots = (2 * slots - (slots & (CAP - 1))).astype(jnp.float32)
    both_ref[...] = jnp.where((slots == places[0]) | (slots == places[1]), 1.0, 0.0).astype(jnp.bfloat16)


def select(place):
    tokens = place.shape[1]
    shape = jax.ShapeDtypeStruct((tokens, tokens * CAP), jnp.bfloat16)
    half = jax.ShapeDtypeStruct((tokens, tokens * CAP // 2), jnp.bfloat16)
    return pl.pallas_call(select_kernel, out_shape=(shape, shape, half), name="select")(place)


def send_cot_kernel(cot_ref, pick_ref, weight_ref, out_ref):
    rows = jnp.dot(pick_ref[...], cot_ref[...], preferred_element_type=jnp.float32)
    rows = (rows * weight_ref[...]).astype(jnp.bfloat16).reshape(-1, CAP, cot_ref.shape[1])
    out_ref[:, 0] = rows
    out_ref[:, 1] = rows


def send_cot(cotangent, pick, slot_weight, steps=4):
    tokens, width = cotangent.shape
    experts = pick.shape[0] // CAP
    return pl.pallas_call(
        send_cot_kernel,
        grid=(steps,),
        in_specs=[
            pl.BlockSpec(cotangent.shape, lambda i: (0, 0)),
            pl.BlockSpec((experts * CAP // steps, tokens), lambda i: (i, 0)),
            pl.BlockSpec((experts * CAP // steps, 1), lambda i: (i, 0)),
        ],
        out_specs=pl.BlockSpec((experts // steps, 2, CAP, width), lambda i: (i, 0, 0, 0)),
        out_shape=jax.ShapeDtypeStruct((experts, 2, CAP, width), jnp.bfloat16),
        compiler_params=pltpu.CompilerParams(vmem_limit_bytes=VMEM_LIMIT),
        cost_estimate=pl.CostEstimate(flops=2 * experts * CAP * tokens * width, bytes_accessed=10_000_000, transcendentals=0),
        name="send_cot",
    )(cotangent, pick, slot_weight)


def finish_out_kernel(back_ref, first_ref, second_ref, weight_ref, cot_ref, out_ref, grad_ref):
    tokens, part = out_ref.shape
    rows = back_ref[...].reshape(-1, part)
    first = jnp.dot(first_ref[...], rows, preferred_element_type=jnp.float32)
    second = jnp.dot(second_ref[...], rows, preferred_element_type=jnp.float32)
    first = first.astype(jnp.bfloat16).astype(jnp.float32)
    second = second.astype(jnp.bfloat16).astype(jnp.float32)
    cot = cot_ref[...].astype(jnp.float32)
    total = first * row_to_column(weight_ref[0:1, :], tokens) + second * row_to_column(weight_ref[1:2, :], tokens)
    out_ref[...] = total.astype(jnp.bfloat16)

    @pl.when(pl.program_id(0) == 0)
    def _():
        grad_ref[...] = jnp.zeros_like(grad_ref)

    grad_ref[0:1, :] += column_to_row(jnp.sum(cot * first, axis=1, keepdims=True), tokens)
    grad_ref[1:2, :] += column_to_row(jnp.sum(cot * second, axis=1, keepdims=True), tokens)


def finish_out(back, first, second, weight, cotangent, steps=4):
    nodes, cap, width = back.shape
    tokens = cotangent.shape[0]
    part = width // steps
    whole = lambda i: (0, 0)
    return pl.pallas_call(
        finish_out_kernel,
        grid=(steps,),
        in_specs=[
            pl.BlockSpec((nodes, cap, part), lambda i: (0, 0, i)),
            pl.BlockSpec(first.shape, whole),
            pl.BlockSpec(second.shape, whole),
            pl.BlockSpec(weight.shape, whole),
            pl.BlockSpec((tokens, part), lambda i: (0, i)),
        ],
        out_specs=(
            pl.BlockSpec((tokens, part), lambda i: (0, i)),
            pl.BlockSpec((2, tokens), whole),
        ),
        out_shape=(
            jax.ShapeDtypeStruct((tokens, width), jnp.bfloat16),
            jax.ShapeDtypeStruct((2, tokens), jnp.float32),
        ),
        compiler_params=pltpu.CompilerParams(vmem_limit_bytes=VMEM_LIMIT),
        cost_estimate=pl.CostEstimate(flops=4 * nodes * cap * tokens * width, bytes_accessed=10_000_000, transcendentals=0),
        name="finish_out",
    )(back, first, second, weight, cotangent)


def finish_in_kernel(back_ref, both_ref, out_ref):
    rows = (back_ref[:, 0].astype(jnp.float32) + back_ref[:, 1].astype(jnp.float32)).astype(jnp.bfloat16)
    rows = rows.reshape(-1, out_ref.shape[1])
    out_ref[...] = jnp.dot(both_ref[...], rows, preferred_element_type=jnp.float32).astype(jnp.bfloat16)


def finish_in(back, both, steps=2):
    nodes, cap, width = back.shape
    tokens = both.shape[0]
    part = width // steps
    return pl.pallas_call(
        finish_in_kernel,
        grid=(steps,),
        in_specs=[
            pl.BlockSpec((nodes // 2, 2, cap, part), lambda i: (0, 0, 0, i)),
            pl.BlockSpec(both.shape, lambda i: (0, 0)),
        ],
        out_specs=pl.BlockSpec((tokens, part), lambda i: (0, i)),
        out_shape=jax.ShapeDtypeStruct((tokens, width), jnp.bfloat16),
        compiler_params=pltpu.CompilerParams(vmem_limit_bytes=VMEM_LIMIT),
        name="finish_in",
    )(back.reshape(nodes // 2, 2, cap, width), both)


def dot(a, b, a_dim, b_dim):
    return lax.dot_general(a, b, (((a_dim,), (b_dim,)), ((), ())), preferred_element_type=jnp.float32)


def exchange(rows):
    return lax.all_to_all(rows, AXES, split_axis=0, concat_axis=0, tiled=True)


def on_device(coded, block_scale, routes, route_weight, cotangent, w_gate, w_up, w_down):
    tokens, width = coded.shape
    nodes = lax.axis_size(AXES)
    weight = route_weight.T
    gate_w, up_w, down_w = w_gate[0].T, w_up[0].T, w_down[0]

    send_rows = send_in(coded, block_scale.T, routes.T)
    rows = exchange(send_rows.reshape(nodes, CAP, width))
    late_routes, _ = lax.optimization_barrier((routes.T, send_rows))
    pick, slot_weight, place = plan(late_routes, weight)
    rows, send_cots = lax.optimization_barrier((rows, send_cot(cotangent, pick, slot_weight)))
    cot_rows = exchange(send_cots.reshape(nodes, CAP, width))
    rows = rows.reshape(-1, width)
    cot_rows = cot_rows.reshape(-1, width)

    gate = dot(rows, gate_w, 1, 1)
    upper = dot(rows, up_w, 1, 1)
    sigma = jax.nn.sigmoid(gate)
    active = gate * sigma
    hidden = (active * upper).astype(jnp.bfloat16)
    partial_out = dot(hidden, down_w, 1, 0).astype(jnp.bfloat16)
    partial_out, cot_rows = lax.optimization_barrier((partial_out, cot_rows))
    back_out = exchange(partial_out.reshape(nodes, CAP, width))

    d_hidden = dot(cot_rows, down_w, 1, 1)
    d_upper = (d_hidden * active).astype(jnp.bfloat16)
    d_gate = (d_hidden * upper * sigma * (1.0 + gate * (1.0 - sigma))).astype(jnp.bfloat16)
    partial_in = (dot(d_gate, gate_w, 1, 0) + dot(d_upper, up_w, 1, 0)).astype(jnp.bfloat16)
    partial_in, back_out = lax.optimization_barrier((partial_in, back_out))
    back_in = exchange(partial_in.reshape(nodes, CAP, width))

    grad_down = dot(hidden, cot_rows, 0, 0).astype(jnp.bfloat16)
    grad_gate = dot(d_gate, rows, 0, 0).astype(jnp.bfloat16)
    grad_up = dot(d_upper, rows, 0, 0).astype(jnp.bfloat16)

    first, second, both = select(place)
    layer_out, grad_weight = finish_out(back_out, first, second, weight, cotangent)
    grad_input = finish_in(back_in, both)
    return (layer_out, grad_input, grad_weight.T, grad_gate.T[None], grad_up.T[None], grad_down[None])


def solution(mesh):
    rows = P(AXES, None)
    matrix = P(AXES, None, None)
    return jax.shard_map(
        on_device,
        mesh=mesh,
        in_specs=(rows, rows, rows, rows, rows, matrix, matrix, matrix),
        out_specs=(rows, rows, rows, matrix, matrix, matrix),
        check_vma=False,
    )
```

```python
import jax
import jax.numpy as jnp
from jax import lax
from jax.experimental import pallas as pl
from jax.experimental.pallas import tpu as pltpu
from jax.sharding import PartitionSpec as P

AXES = ("dp", "expert")
CAP = 8
PARTS = 4
VMEM_LIMIT = 60 * 1024 * 1024


def row_to_column(row, size):
    eye = lax.broadcasted_iota(jnp.int32, (size, size), 0) == lax.broadcasted_iota(jnp.int32, (size, size), 1)
    return jnp.sum(jnp.where(eye, row, 0.0), axis=1, keepdims=True)


def column_to_row(column, size):
    eye = lax.broadcasted_iota(jnp.int32, (size, size), 0) == lax.broadcasted_iota(jnp.int32, (size, size), 1)
    return jnp.sum(jnp.where(eye, column, 0.0), axis=0, keepdims=True)


def pick_rows(routes_ref, experts, tokens):
    numbers = lax.broadcasted_iota(jnp.int32, (experts, tokens), 0)
    first = routes_ref[0:1, :] == numbers
    second = routes_ref[1:2, :] == numbers
    named = jnp.where(first | second, 1.0, 0.0)
    earlier = lax.broadcasted_iota(jnp.int32, (tokens, tokens), 0) < lax.broadcasted_iota(jnp.int32, (tokens, tokens), 1)
    rank = jnp.dot(
        named.astype(jnp.bfloat16),
        jnp.where(earlier, 1.0, 0.0).astype(jnp.bfloat16),
        preferred_element_type=jnp.float32,
    )
    slots = lax.broadcasted_iota(jnp.int32, (experts, CAP, tokens), 1).astype(jnp.float32)
    slot_of = jnp.where(named > 0.0, rank, -1.0)
    pick = jnp.broadcast_to(slot_of[:, None, :], (experts, CAP, tokens)) == slots
    return pick, first, second, rank


def as_matrix(pick):
    experts, cap, tokens = pick.shape
    return jnp.where(pick, 1.0, 0.0).astype(jnp.bfloat16).reshape(experts * cap, tokens)


def send_in_kernel(coded_hbm, scale_hbm, routes_hbm, out_hbm, coded_ref, rows_ref, scale_ref, routes_ref, in_sem, out_sem):
    tokens, width = coded_ref.shape
    blocks = scale_ref.shape[0]
    size = width // blocks
    experts = tokens // 2
    copy_routes = pltpu.make_async_copy(routes_hbm, routes_ref, in_sem.at[0])
    copy_routes.start()
    copy_scale = pltpu.make_async_copy(scale_hbm, scale_ref, in_sem.at[1])
    copy_scale.start()
    copy_coded = pltpu.make_async_copy(coded_hbm, coded_ref, in_sem.at[2])
    copy_coded.start()
    copy_routes.wait()
    pick = as_matrix(pick_rows(routes_ref, experts, tokens)[0])
    copy_scale.wait()
    scales = [row_to_column(scale_ref[b : b + 1, :], tokens) for b in range(blocks)]
    copy_coded.wait()
    for b in range(blocks):
        columns = pl.ds(b * size, size)
        coded_ref[:, columns] = (coded_ref[:, columns].astype(jnp.float32) * scales[b]).astype(jnp.bfloat16)
    copies = []
    deep = experts // PARTS
    for k in range(PARTS):
        rows = jnp.dot(pick[k * deep * CAP : (k + 1) * deep * CAP], coded_ref[...], preferred_element_type=jnp.float32)
        rows_ref[k * deep : (k + 1) * deep] = rows.astype(jnp.bfloat16).reshape(deep, CAP, width)
        for half in range(2):
            copy = pltpu.make_async_copy(rows_ref.at[pl.ds(k * deep, deep)], out_hbm.at[pl.ds(k * deep, deep), half], out_sem.at[k, half])
            copy.start()
            copies.append(copy)
    for copy in copies:
        copy.wait()


def send_in(coded, scale, routes):
    tokens, width = coded.shape
    experts = tokens // 2
    hbm = pl.BlockSpec(memory_space=pl.ANY)
    return pl.pallas_call(
        send_in_kernel,
        in_specs=[hbm, hbm, hbm],
        out_specs=hbm,
        out_shape=jax.ShapeDtypeStruct((experts, 2, CAP, width), jnp.bfloat16),
        scratch_shapes=[
            pltpu.VMEM((tokens, width), jnp.bfloat16),
            pltpu.VMEM((experts, CAP, width), jnp.bfloat16),
            pltpu.VMEM(scale.shape, jnp.float32),
            pltpu.VMEM(routes.shape, jnp.int32),
            pltpu.SemaphoreType.DMA((3,)),
            pltpu.SemaphoreType.DMA((PARTS, 2)),
        ],
        compiler_params=pltpu.CompilerParams(vmem_limit_bytes=VMEM_LIMIT),
        name="send_in",
    )(coded, scale, routes)


def plan_kernel(routes_ref, weight_ref, pick_ref, slot_weight_ref, place_ref):
    tokens = routes_ref.shape[1]
    experts = tokens // 2
    pick, first, second, rank = pick_rows(routes_ref, experts, tokens)
    pick_ref[...] = as_matrix(pick)
    weight = jnp.where(first, weight_ref[0:1, :], 0.0) + jnp.where(second, weight_ref[1:2, :], 0.0)
    spread = jnp.broadcast_to(weight[:, None, :], pick.shape)
    slot_weight_ref[...] = jnp.sum(jnp.where(pick, spread, 0.0).reshape(experts * CAP, tokens), axis=1, keepdims=True)
    place = lax.broadcasted_iota(jnp.int32, (experts, tokens), 0).astype(jnp.float32) * (2 * CAP) + rank
    place_ref[0:1, :] = jnp.sum(jnp.where(first, place, 0.0), axis=0, keepdims=True)
    place_ref[1:2, :] = jnp.sum(jnp.where(second, place, 0.0), axis=0, keepdims=True)


def plan(routes, weight):
    tokens = routes.shape[1]
    experts = tokens // 2
    return pl.pallas_call(
        plan_kernel,
        out_shape=(
            jax.ShapeDtypeStruct((experts * CAP, tokens), jnp.bfloat16),
            jax.ShapeDtypeStruct((experts * CAP, 1), jnp.float32),
            jax.ShapeDtypeStruct((2, tokens), jnp.float32),
        ),
        compiler_params=pltpu.CompilerParams(vmem_limit_bytes=VMEM_LIMIT),
        name="plan",
    )(routes, weight)


def select_kernel(place_ref, first_ref, second_ref, both_ref):
    tokens = place_ref.shape[1]
    rows = first_ref.shape[1]
    numbers = lax.broadcasted_iota(jnp.int32, (tokens, rows), 1)
    numbers = (numbers - jnp.where((numbers & CAP) != 0, CAP, 0)).astype(jnp.float32)
    first = jnp.where(numbers == row_to_column(place_ref[0:1, :], tokens), 1.0, 0.0)
    second = jnp.where(numbers == row_to_column(place_ref[1:2, :], tokens), 1.0, 0.0)
    first_ref[...] = first.astype(jnp.bfloat16)
    second_ref[...] = second.astype(jnp.bfloat16)
    both_ref[...] = (first + second).astype(jnp.bfloat16)


def select(place):
    tokens = place.shape[1]
    shape = jax.ShapeDtypeStruct((tokens, tokens * CAP), jnp.bfloat16)
    return pl.pallas_call(select_kernel, out_shape=(shape,) * 3, name="select")(place)


def send_cot_kernel(cot_ref, pick_ref, weight_ref, out_ref):
    rows = jnp.dot(pick_ref[...], cot_ref[...], preferred_element_type=jnp.float32)
    rows = (rows * weight_ref[...]).astype(jnp.bfloat16).reshape(-1, CAP, cot_ref.shape[1])
    out_ref[:, 0] = rows
    out_ref[:, 1] = rows


def send_cot(cotangent, pick, slot_weight, steps=4):
    tokens, width = cotangent.shape
    experts = pick.shape[0] // CAP
    return pl.pallas_call(
        send_cot_kernel,
        grid=(steps,),
        in_specs=[
            pl.BlockSpec(cotangent.shape, lambda i: (0, 0)),
            pl.BlockSpec((experts * CAP // steps, tokens), lambda i: (i, 0)),
            pl.BlockSpec((experts * CAP // steps, 1), lambda i: (i, 0)),
        ],
        out_specs=pl.BlockSpec((experts // steps, 2, CAP, width), lambda i: (i, 0, 0, 0)),
        out_shape=jax.ShapeDtypeStruct((experts, 2, CAP, width), jnp.bfloat16),
        compiler_params=pltpu.CompilerParams(vmem_limit_bytes=VMEM_LIMIT),
        cost_estimate=pl.CostEstimate(flops=2 * experts * CAP * tokens * width, bytes_accessed=10_000_000, transcendentals=0),
        name="send_cot",
    )(cotangent, pick, slot_weight)


def finish_out_kernel(back_ref, first_ref, second_ref, weight_ref, cot_ref, out_ref, grad_ref):
    tokens, part = out_ref.shape
    rows = back_ref[...].reshape(-1, part)
    first = jnp.dot(first_ref[...], rows, preferred_element_type=jnp.float32)
    second = jnp.dot(second_ref[...], rows, preferred_element_type=jnp.float32)
    first = first.astype(jnp.bfloat16).astype(jnp.float32)
    second = second.astype(jnp.bfloat16).astype(jnp.float32)
    cot = cot_ref[...].astype(jnp.float32)
    total = first * row_to_column(weight_ref[0:1, :], tokens) + second * row_to_column(weight_ref[1:2, :], tokens)
    out_ref[...] = total.astype(jnp.bfloat16)

    @pl.when(pl.program_id(0) == 0)
    def _():
        grad_ref[...] = jnp.zeros_like(grad_ref)

    grad_ref[0:1, :] += column_to_row(jnp.sum(cot * first, axis=1, keepdims=True), tokens)
    grad_ref[1:2, :] += column_to_row(jnp.sum(cot * second, axis=1, keepdims=True), tokens)


def finish_out(back, first, second, weight, cotangent, steps=4):
    nodes, cap, width = back.shape
    tokens = cotangent.shape[0]
    part = width // steps
    whole = lambda i: (0, 0)
    return pl.pallas_call(
        finish_out_kernel,
        grid=(steps,),
        in_specs=[
            pl.BlockSpec((nodes, cap, part), lambda i: (0, 0, i)),
            pl.BlockSpec(first.shape, whole),
            pl.BlockSpec(second.shape, whole),
            pl.BlockSpec(weight.shape, whole),
            pl.BlockSpec((tokens, part), lambda i: (0, i)),
        ],
        out_specs=(
            pl.BlockSpec((tokens, part), lambda i: (0, i)),
            pl.BlockSpec((2, tokens), whole),
        ),
        out_shape=(
            jax.ShapeDtypeStruct((tokens, width), jnp.bfloat16),
            jax.ShapeDtypeStruct((2, tokens), jnp.float32),
        ),
        compiler_params=pltpu.CompilerParams(vmem_limit_bytes=VMEM_LIMIT),
        cost_estimate=pl.CostEstimate(flops=4 * nodes * cap * tokens * width, bytes_accessed=10_000_000, transcendentals=0),
        name="finish_out",
    )(back, first, second, weight, cotangent)


def finish_in_kernel(back_ref, both_ref, out_ref):
    rows = back_ref[...].reshape(-1, out_ref.shape[1])
    out_ref[...] = jnp.dot(both_ref[...], rows, preferred_element_type=jnp.float32).astype(jnp.bfloat16)


def finish_in(back, both, steps=2):
    nodes, cap, width = back.shape
    tokens = both.shape[0]
    part = width // steps
    return pl.pallas_call(
        finish_in_kernel,
        grid=(steps,),
        in_specs=[
            pl.BlockSpec((nodes, cap, part), lambda i: (0, 0, i)),
            pl.BlockSpec(both.shape, lambda i: (0, 0)),
        ],
        out_specs=pl.BlockSpec((tokens, part), lambda i: (0, i)),
        out_shape=jax.ShapeDtypeStruct((tokens, width), jnp.bfloat16),
        compiler_params=pltpu.CompilerParams(vmem_limit_bytes=VMEM_LIMIT),
        name="finish_in",
    )(back, both)


def dot(a, b, a_dim, b_dim):
    return lax.dot_general(a, b, (((a_dim,), (b_dim,)), ((), ())), preferred_element_type=jnp.float32)


def exchange(rows):
    return lax.all_to_all(rows, AXES, split_axis=0, concat_axis=0, tiled=True)


def on_device(coded, block_scale, routes, route_weight, cotangent, w_gate, w_up, w_down):
    tokens, width = coded.shape
    nodes = lax.axis_size(AXES)
    weight = route_weight.T
    gate_w, up_w, down_w = w_gate[0].T, w_up[0].T, w_down[0]

    send_rows = send_in(coded, block_scale.T, routes.T)
    rows = exchange(send_rows.reshape(nodes, CAP, width))
    late_routes, down_w, _ = lax.optimization_barrier((routes.T, down_w, send_rows))
    pick, slot_weight, place = plan(late_routes, weight)
    rows, send_cots = lax.optimization_barrier((rows, send_cot(cotangent, pick, slot_weight)))
    cot_rows = exchange(send_cots.reshape(nodes, CAP, width))
    rows = rows.reshape(-1, width)
    cot_rows = cot_rows.reshape(-1, width)

    gate = dot(rows, gate_w, 1, 1)
    upper = dot(rows, up_w, 1, 1)
    sigma = jax.nn.sigmoid(gate)
    active = gate * sigma
    hidden = (active * upper).astype(jnp.bfloat16)
    partial_out = dot(hidden, down_w, 1, 0).astype(jnp.bfloat16)
    partial_out, cot_rows = lax.optimization_barrier((partial_out, cot_rows))
    back_out = exchange(partial_out.reshape(nodes, CAP, width))

    d_hidden = dot(cot_rows, down_w, 1, 1)
    d_upper = (d_hidden * active).astype(jnp.bfloat16)
    d_gate = (d_hidden * upper * sigma * (1.0 + gate * (1.0 - sigma))).astype(jnp.bfloat16)
    partial_in = (dot(d_gate, gate_w, 1, 0) + dot(d_upper, up_w, 1, 0)).astype(jnp.bfloat16)
    partial_in, back_out = lax.optimization_barrier((partial_in, back_out))
    back_in = exchange(partial_in.reshape(nodes, CAP, width))

    grad_down = dot(hidden, cot_rows, 0, 0).astype(jnp.bfloat16)
    grad_gate = dot(d_gate, rows, 0, 0).astype(jnp.bfloat16)
    grad_up = dot(d_upper, rows, 0, 0).astype(jnp.bfloat16)

    first, second, both = select(place)
    layer_out, grad_weight = finish_out(back_out, first, second, weight, cotangent)
    grad_input = finish_in(back_in, both)
    return (layer_out, grad_input, grad_weight.T, grad_gate.T[None], grad_up.T[None], grad_down[None])


def solution(mesh):
    rows = P(AXES, None)
    matrix = P(AXES, None, None)
    return jax.shard_map(
        on_device,
        mesh=mesh,
        in_specs=(rows, rows, rows, rows, rows, matrix, matrix, matrix),
        out_specs=(rows, rows, rows, matrix, matrix, matrix),
        check_vma=False,
    )
```
